32 devices in a mesh: layer: 4 (over y, core), blk: 8 (over z, x).
Axes of the slice: x: 2, y: 2, z: 4, core: 2. Of those that a mesh axis runs over, the one named last changes fastest.
Arguments:
- source: bfloat16 [4, 2, 128, 32768], P('layer', None, None, 'blk'), may hold values from -6 to 6
- tile_data: bfloat16 [4, 192, 2, 512, 512], P('layer', 'blk'), may hold values from -0.078125 to 0.078125
- tile_rows: int32 [4, 192], P('layer', 'blk'), may hold values from 0 to 63, as said below
- tile_cols: int32 [4, 192], P('layer', 'blk'), may hold values from 0 to 63, as said below
- tile_count: int32 [4, 8], P('layer', 'blk'), may hold values from 10 to 24, as said below
Outputs:
- down_trace: bfloat16 [4, 2, 128, 32768], P('layer', None, None, 'blk')
- up_trace: bfloat16 [4, 2, 128, 32768], P('layer', None, None, 'blk')
The draws below stay inside these ranges and needn't reach their ends.
Inputs may be any that keep to these rules, and one draw needn't show every extreme that they name: `tile_rows`: every slot of row range g (slots g*24 to (g+1)*24 - 1) has its row block in g*8 to (g+1)*8 - 1; the live slots of one range hold distinct tiles in shuffled order, among them the diagonal tile of each of its row blocks, and the tile one block left of its first row block and one block right of its last where those exist. Slots that are not live also hold valid indices. `tile_cols`: every slot's column block lies within 2 blocks of its row block, inside the grid. `tile_count`: in every section some row range has all 24 slots live.
All inputs are finite; a program needn't handle non-finite values.
Results may differ from the reference program's by a relative error of at most 0.01.
Values may be sent and summed in bfloat16 or wider, within the bound.
A program may use at most 64 MiB of HBM per device.

```python
import jax
import jax.numpy as jnp
from jax import lax

TILE = 512
ROWS = 32768
BAND = 2
LAYERS = 4
COLS = 128
ROW_BLOCKS = 64
RB_DEV = 8
SLOTS = 24
N_LAYER = 4
N_BLK = 8


def tile_lists(key):
    groups = ROW_BLOCKS // RB_DEV
    cand_n = 4 * RB_DEV
    offsets = jnp.array([-2, -1, 1, 2], jnp.int32)
    group_ids = jnp.arange(groups, dtype=jnp.int32)
    own_rows = group_ids[:, None] * RB_DEV + jnp.arange(RB_DEV, dtype=jnp.int32)[None, :]
    cand_rows = jnp.repeat(own_rows, 4, axis=1)
    offset_all = jnp.tile(offsets, RB_DEV)
    local_pos = jnp.repeat(jnp.arange(RB_DEV, dtype=jnp.int32), 4)
    cand_cols = cand_rows + offset_all[None, :]
    usable = (cand_cols >= 0) & (cand_cols < ROW_BLOCKS)
    forced = usable & ((local_pos == 0) & (offset_all == -1) | (local_pos == RB_DEV - 1) & (offset_all == 1))[None, :]
    subkeys = jax.random.split(jax.random.fold_in(key, 7), 4)
    jitter = jax.random.randint(subkeys[0], (N_LAYER, groups, cand_n), 0, 1 << 16)
    ranking = jnp.where(forced[None], 0, jnp.where(usable[None], 1 + jitter, 1 << 17))
    ordering = jnp.argsort(ranking * cand_n + jnp.arange(cand_n, dtype=jnp.int32), axis=-1)
    extra_n = SLOTS - RB_DEV
    picked = ordering[..., :extra_n]
    wide_rows = jnp.broadcast_to(cand_rows[None], (N_LAYER, groups, cand_n))
    wide_cols = jnp.broadcast_to(cand_cols[None], (N_LAYER, groups, cand_n))
    extra_rows = jnp.take_along_axis(wide_rows, picked, axis=-1)
    extra_cols = jnp.take_along_axis(wide_cols, picked, axis=-1)
    diag_rows = jnp.broadcast_to(own_rows[None], (N_LAYER, groups, RB_DEV))
    slot_rows = jnp.concatenate([diag_rows, extra_rows], axis=-1)
    slot_cols = jnp.concatenate([diag_rows, extra_cols], axis=-1)
    counts = jax.random.randint(subkeys[1], (N_LAYER, groups), RB_DEV + 2, SLOTS + 1)
    fullest = jax.random.randint(subkeys[2], (N_LAYER, 1), 0, groups)
    counts = jnp.where(group_ids[None, :] == fullest, SLOTS, counts).astype(jnp.int32)
    slot_pos = jnp.arange(SLOTS, dtype=jnp.int32)
    shuffle_jitter = jax.random.randint(subkeys[3], (N_LAYER, groups, SLOTS), 0, 1 << 16)
    shuffle_rank = jnp.where(slot_pos[None, None, :] < counts[..., None], shuffle_jitter, (1 << 17) + slot_pos[None, None, :])
    shuffle = jnp.argsort(shuffle_rank * SLOTS + slot_pos[None, None, :], axis=-1)
    slot_rows = jnp.take_along_axis(slot_rows, shuffle, axis=-1)
    slot_cols = jnp.take_along_axis(slot_cols, shuffle, axis=-1)
    return (slot_rows.reshape(N_LAYER, groups * SLOTS).astype(jnp.int32), slot_cols.reshape(N_LAYER, groups * SLOTS).astype(jnp.int32), counts)


def draw_tile_rows(key, part):
    return tile_lists(key)[0]


def draw_tile_cols(key, part):
    return tile_lists(key)[1]


def draw_tile_count(key, part):
    return tile_lists(key)[2]


def block_scale(rng, shape, cuts, least, high):
    def one(position, blocks):
        steps = jax.random.uniform(jax.random.fold_in(jax.random.fold_in(rng, 6), position), (blocks,), jnp.float32, least / len(cuts), high / len(cuts))
        return jnp.repeat(jnp.exp(steps), shape[position] // blocks).reshape((-1,) + (1,) * (len(shape) - position - 1))

    level = one(*cuts[0])
    for cut in cuts[1:]:
        level = level * one(*cut)
    return level


def normal_values(rng, shape, deviation, most, cuts=(), held_as=jnp.bfloat16):
    drawn = deviation * jax.random.normal(rng, shape, jnp.float32)
    if cuts:
        drawn = drawn * block_scale(rng, shape, cuts, -0.22, 0.18)
    return jnp.clip(drawn, -most, most).astype(held_as)


def setup_inputs(seed: int = 0) -> dict:
    keys = jax.random.split(jax.random.key(seed), 6)
    source = normal_values(keys[0], (LAYERS, 2, COLS, ROWS), 1.0, 6.0, ((0, 4), (3, 8)))
    tile_data = normal_values(keys[1], (LAYERS, N_BLK * SLOTS, 2, TILE, TILE), (12 * TILE) ** -0.5, 0.078125, ((0, 4), (1, 8)))
    tile_rows = draw_tile_rows(jax.random.fold_in(keys[5], 71), 0)
    tile_cols = draw_tile_cols(jax.random.fold_in(keys[5], 71), 0)
    tile_count = draw_tile_count(jax.random.fold_in(keys[5], 71), 0)
    return dict(source=source, tile_data=tile_data, tile_rows=tile_rows, tile_cols=tile_cols, tile_count=tile_count)


def complex_apply(segment, matrix, contract):
    halves = segment.shape[1]
    flattened = segment.reshape(2 * halves, segment.shape[2])
    numbers = (((1,), (contract,)), ((), ()))
    with_real = lax.dot_general(flattened, matrix[0], numbers, precision=lax.Precision.HIGHEST, preferred_element_type=jnp.float32)
    with_imag = lax.dot_general(flattened, matrix[1], numbers, precision=lax.Precision.HIGHEST, preferred_element_type=jnp.float32)
    return jnp.stack((with_real[:halves] - with_imag[halves:], with_imag[:halves] + with_real[halves:]))


def live_slots(tile_count, layer_index):
    groups = tile_count.shape[1]
    slot_ids = jnp.arange(groups * SLOTS, dtype=jnp.int32)
    return (slot_ids % SLOTS) < jnp.repeat(tile_count[layer_index], SLOTS)


def apply_down(tile_layer, rows_layer, cols_layer, usable, current):
    values = current.astype(jnp.float32)

    def one_slot(summed, inputs):
        matrix, row_block, col_block, is_live = inputs
        segment = lax.dynamic_slice_in_dim(values, col_block * TILE, TILE, 2)
        product = complex_apply(segment, matrix.astype(jnp.float32), 1)
        start_row = row_block * TILE
        target = lax.dynamic_slice_in_dim(summed, start_row, TILE, 2)
        return lax.dynamic_update_slice_in_dim(summed, target + jnp.where(is_live, product, 0.0), start_row, 2), None

    summed, ignored = lax.scan(one_slot, jnp.zeros(values.shape, jnp.float32), (tile_layer, rows_layer, cols_layer, usable))
    return summed


def apply_up(tile_layer, rows_layer, cols_layer, usable, current):
    groups = rows_layer.shape[0] // SLOTS
    rows_dev = ROWS // groups
    margin = BAND * TILE
    values = current.astype(jnp.float32)
    columns = values.shape[1]
    positions = jnp.arange(rows_dev + 2 * margin, dtype=jnp.int32)
    inside = (positions >= margin) & (positions < margin + rows_dev)

    def one_group(padded, inputs):
        group_tiles, group_rows, group_cols, group_live, group_index = inputs
        first_row = group_index * rows_dev

        def one_slot(extended, slot_inputs):
            matrix, row_block, col_block, is_live = slot_inputs
            segment = lax.dynamic_slice_in_dim(values, row_block * TILE, TILE, 2)
            product = complex_apply(segment, matrix.astype(jnp.float32), 0)
            placed_at = col_block * TILE - first_row + margin
            target = lax.dynamic_slice_in_dim(extended, placed_at, TILE, 2)
            return lax.dynamic_update_slice_in_dim(extended, target + jnp.where(is_live, product, 0.0), placed_at, 2), None

        extended, ignored = lax.scan(one_slot, jnp.zeros((2, columns, rows_dev + 2 * margin), jnp.float32), (group_tiles, group_rows, group_cols, group_live))
        narrowed = lax.optimization_barrier(extended.astype(jnp.bfloat16)).astype(jnp.float32)
        shared = jnp.where(inside, extended, narrowed)
        target = lax.dynamic_slice_in_dim(padded, first_row, rows_dev + 2 * margin, 2)
        return lax.dynamic_update_slice_in_dim(padded, target + shared, first_row, 2), None

    padded, ignored = lax.scan(
        one_group,
        jnp.zeros((2, columns, ROWS + 2 * margin), jnp.float32),
        (tile_layer.reshape(groups, SLOTS, 2, TILE, TILE), rows_layer.reshape(groups, SLOTS), cols_layer.reshape(groups, SLOTS), usable.reshape(groups, SLOTS), jnp.arange(groups, dtype=jnp.int32)),
    )
    return padded[:, :, margin:margin + ROWS]


def reference(source, tile_data, tile_rows, tile_cols, tile_count):
    down_list = []
    forward = None
    for layer_index in range(N_LAYER):
        if layer_index == 0:
            current = source[0]
        else:
            current = (source[layer_index].astype(jnp.float32) + forward.astype(jnp.float32)).astype(jnp.bfloat16)
        down_list.append(current)
        if layer_index + 1 < N_LAYER:
            forward = apply_down(tile_data[layer_index], tile_rows[layer_index], tile_cols[layer_index], live_slots(tile_count, layer_index), current).astype(jnp.bfloat16)
    up_list = [None] * N_LAYER
    backward = None
    for layer_index in reversed(range(N_LAYER)):
        if layer_index == N_LAYER - 1:
            current = down_list[layer_index]
        else:
            current = (down_list[layer_index].astype(jnp.float32) + backward.astype(jnp.float32)).astype(jnp.bfloat16)
        up_list[layer_index] = current
        if layer_index > 0:
            backward = apply_up(tile_data[layer_index], tile_rows[layer_index], tile_cols[layer_index], live_slots(tile_count, layer_index), current).astype(jnp.bfloat16)
    return jnp.stack(down_list), jnp.stack(up_list)
```

```python
import functools

import jax
import jax.numpy as jnp
from jax import lax
from jax.experimental import pallas as pl
from jax.experimental.pallas import tpu as pltpu
from jax.sharding import PartitionSpec as P

BAND = 2
MESH = pl.DeviceIdType.MESH


def block_order(n):
    if n <= 2 * BAND:
        return list(range(n))
    return list(range(BAND)) + list(range(n - BAND, n)) + list(range(BAND, n - BAND))


def sorted_by(key, values):
    rank = jnp.sum(key[None, :] < key[:, None], axis=1)
    slots = key.shape[0]
    place = rank[None, :] == jnp.arange(slots)[:, None]
    return [jnp.sum(jnp.where(place, v[None, :], 0), axis=1) for v in values]


def chain(group, alive, first, base, groups):
    slots = group.shape[0]
    at = jnp.arange(slots, dtype=jnp.int32)
    same = jnp.concatenate([jnp.zeros((1,), bool), (group[1:] == group[:-1]) & (alive[1:] > 0)])
    prev = jnp.where(same, base + at - 1, first(group))
    member = (group[None, :] == jnp.arange(groups)[:, None]) & (alive[None, :] > 0)
    last = jnp.max(jnp.where(member, base + at[None, :], -1), axis=1)
    return prev, last


def plan(rows, cols, count, first_block, n):
    slots = rows.shape[0]
    ids = jnp.arange(slots, dtype=jnp.int32)
    r = rows - first_block
    c = cols - first_block + BAND
    live = ids < count
    diag = live & (c == r + BAND)
    dslot = jnp.sum(
        jnp.where(diag[None, :] & (r[None, :] == jnp.arange(n)[:, None]), ids[None, :], 0), axis=1
    )
    order = block_order(n)
    prio_r = [0] * n
    for p, b in enumerate(order):
        prio_r[b] = p
    rank_r = sum(jnp.where(r == b, prio_r[b], 0) for b in range(n))
    big = 64 * slots
    key = jnp.where(diag, 2 * big, jnp.where(live, rank_r * slots, big)) + ids
    s_ids, s_r, s_c, s_live = sorted_by(key, [ids, r, c, live.astype(jnp.int32)])
    rest = slots - n
    d_ord, d_r, d_c, d_live = s_ids[:rest], s_r[:rest], s_c[:rest], s_live[:rest]
    d_prev, d_last = chain(d_r, d_live, lambda g: g, n, n)
    d_last = jnp.where(d_last < 0, jnp.arange(n), d_last)
    wide = n + 2 * BAND
    order_c = list(range(BAND)) + list(range(wide - BAND, wide))
    order_c += [b for b in range(2 * BAND, n)] + [
        b for b in range(BAND, n + BAND) if not 2 * BAND <= b < n
    ]
    prio_c = [0] * wide
    for p, b in enumerate(order_c):
        prio_c[b] = p
    rank_c = sum(jnp.where(c == b, prio_c[b], 0) for b in range(wide))
    key = jnp.where(live, rank_c * slots, big) + ids
    u_ord, u_row, u_col, u_live = sorted_by(key, [ids, r, c, live.astype(jnp.int32)])
    u_prev, u_last = chain(u_col, u_live, lambda g: jnp.full_like(g, slots), 0, wide)
    u_last = jnp.where(u_last < 0, slots, u_last)
    parts = [dslot, d_ord, d_c, d_prev, d_last, u_ord, u_row, u_prev, u_last]
    offsets, at = [], 0
    for p in parts:
        offsets.append(at)
        at += p.shape[0]
    return jnp.concatenate([p.astype(jnp.int32) for p in parts]), offsets


def kernel(
    layers, groups, n, slots, offsets,
    idx, source, tiles_hbm, down_out, up_out,
    tiles, acc, src, ext, up, inc, binc, snd, bsnd, rim_snd, rim_rcv,
    tile_sem, src_sem, out_sem, inc_send, inc_recv, binc_send, binc_recv,
    halo_send, halo_recv, rim_send, rim_recv,
):
    o_dslot, o_dord, o_dcol, o_dprev, o_dlast, o_uord, o_urow, o_uprev, o_ulast = offsets
    half, tile = src.shape[2], src.shape[3]
    layer = lax.axis_index("layer")
    blk = lax.axis_index("blk")
    has_prev, has_next = layer > 0, layer < layers - 1
    has_left, has_right = blk > 0, blk < groups - 1
    to_prev, to_next = (layer - 1, blk), (layer + 1, blk)
    to_left, to_right = (layer, blk - 1), (layer, blk + 1)
    partners = ((has_prev, to_prev), (has_next, to_next), (has_left, to_left), (has_right, to_right))

    def tile_copy(s):
        return pltpu.make_async_copy(tiles_hbm.at[s], tiles.at[s], tile_sem.at[s])

    def src_copy(b):
        return pltpu.make_async_copy(
            source.at[:, :, pl.ds(b * tile, tile)], src.at[b], src_sem.at[b]
        )

    def down_copy(b):
        return pltpu.make_async_copy(
            ext.at[BAND + b], down_out.at[:, :, pl.ds(b * tile, tile)], out_sem.at[0, b]
        )

    def up_copy(b):
        return pltpu.make_async_copy(
            up.at[b], up_out.at[:, :, pl.ds(b * tile, tile)], out_sem.at[1, b]
        )

    def fwd_copy(b):
        return pltpu.make_async_remote_copy(
            src_ref=snd.at[b], dst_ref=inc.at[b], send_sem=inc_send.at[b],
            recv_sem=inc_recv.at[b], device_id=to_next, device_id_type=MESH,
        )

    def bwd_copy(b):
        return pltpu.make_async_remote_copy(
            src_ref=bsnd.at[b], dst_ref=binc.at[b], send_sem=binc_send.at[b],
            recv_sem=binc_recv.at[b], device_id=to_prev, device_id_type=MESH,
        )

    def halo_copy(side):
        if side == 0:
            a, b, dev = ext.at[pl.ds(BAND, BAND)], ext.at[pl.ds(BAND + n, BAND)], to_left
        else:
            a, b, dev = ext.at[pl.ds(n, BAND)], ext.at[pl.ds(0, BAND)], to_right
        return pltpu.make_async_remote_copy(
            src_ref=a, dst_ref=b, send_sem=halo_send.at[side],
            recv_sem=halo_recv.at[side], device_id=dev, device_id_type=MESH,
        )

    def rim_copy(side):
        return pltpu.make_async_remote_copy(
            src_ref=rim_snd.at[side], dst_ref=rim_rcv.at[side], send_sem=rim_send.at[side],
            recv_sem=rim_recv.at[side], device_id=(to_left, to_right)[side], device_id_type=MESH,
        )

    for b in block_order(n):
        src_copy(b).start()

    @pl.loop(0, slots)
    def _(s):
        tile_copy(s).start()

    barrier = pltpu.get_barrier_semaphore()
    for there, dev in partners:
        @pl.when(there)
        def _(dev=dev):
            pl.semaphore_signal(barrier, inc=1, device_id=dev, device_id_type=MESH)
    pl.semaphore_wait(barrier, sum(there.astype(jnp.int32) for there, _ in partners))

    def product(x, s, dim, write):
        x1 = x.reshape(2 * half, tile)
        x2 = jnp.concatenate([-x[1], x[0]], axis=0)
        numbers = (((1,), (dim,)), ((), ()))
        step = min(tile, 256)
        for j in range(0, tile, step):
            if dim == 1:
                real, imag = tiles[s, 0, j:j + step, :], tiles[s, 1, j:j + step, :]
            else:
                real, imag = tiles[s, 0, :, j:j + step], tiles[s, 1, :, j:j + step]
            y = lax.dot_general(x1, real, numbers, preferred_element_type=jnp.float32)
            y = y + lax.dot_general(x2, imag, numbers, preferred_element_type=jnp.float32)
            write(slice(j, j + step), y)

    @pl.when(jnp.logical_not(has_left))
    def _():
        ext[0:BAND] = jnp.zeros((BAND,) + ext.shape[1:], ext.dtype)
        rim_rcv[1] = jnp.zeros(rim_rcv.shape[1:], rim_rcv.dtype)

    @pl.when(jnp.logical_not(has_right))
    def _():
        ext[BAND + n:] = jnp.zeros((BAND,) + ext.shape[1:], ext.dtype)
        rim_rcv[0] = jnp.zeros(rim_rcv.shape[1:], rim_rcv.dtype)

    for p, b in enumerate(block_order(n)):
        src_copy(b).wait()

        @pl.when(has_prev)
        def _(b=b):
            fwd_copy(b).wait_recv()
            total = src[b].astype(jnp.float32) + inc[b].astype(jnp.float32)
            ext[BAND + b] = total.astype(jnp.bfloat16)

        @pl.when(jnp.logical_not(has_prev))
        def _(b=b):
            ext[BAND + b] = src[b]

        if p == min(n, 2 * BAND) - 1:
            for side, there in enumerate((has_left, has_right)):
                @pl.when(has_next & there)
                def _(side=side):
                    halo_copy(side).start()
        down_copy(b).start()

    @pl.loop(0, slots)
    def _(s):
        tile_copy(s).wait()

    @pl.when(has_next)
    def _():
        @pl.loop(0, n)
        def _(r):
            def write(at, y):
                acc[r, :, at] = y

            product(ext[BAND + r], idx[o_dslot + r], 1, write)

        for side, there in enumerate((has_right, has_left)):
            @pl.when(there)
            def _(side=side):
                halo_copy(side).wait_recv()

        @pl.loop(0, slots - n)
        def _(k):
            before = idx[o_dprev + k]

            def write(at, y):
                acc[n + k, :, at] = acc[before, :, at] + y

            product(ext[idx[o_dcol + k]], idx[o_dord + k], 1, write)

        for b in block_order(n):
            snd[b] = acc[idx[o_dlast + b]].astype(jnp.bfloat16).reshape(snd.shape[1:])
            fwd_copy(b).start()

    for b in range(n):
        @pl.when(has_next)
        def _(b=b):
            bwd_copy(b).wait_recv()
            total = ext[BAND + b].astype(jnp.float32) + binc[b].astype(jnp.float32)
            up[b] = total.astype(jnp.bfloat16)

        @pl.when(jnp.logical_not(has_next))
        def _(b=b):
            up[b] = ext[BAND + b]

        up_copy(b).start()

    @pl.when(has_prev)
    def _():
        acc[slots] = jnp.zeros(acc.shape[1:], acc.dtype)

        def slot(k):
            before = idx[o_uprev + k]

            def write(at, y):
                acc[k, :, at] = acc[before, :, at] + y

            product(up[idx[o_urow + k]], idx[o_uord + k], 0, write)

        rims = min(slots, BAND * (BAND + 1))
        pl.loop(0, rims)(slot)
        for side, there in enumerate((has_left, has_right)):
            for b in range(BAND):
                c = b if side == 0 else BAND + n + b
                rim_snd[side, b] = (
                    acc[idx[o_ulast + c]].astype(jnp.bfloat16).reshape(rim_snd.shape[2:])
                )

            @pl.when(there)
            def _(side=side):
                rim_copy(side).start()
        pl.loop(rims, slots)(slot)
        inside = [b for b in range(n) if BAND <= b < n - BAND]
        border = [b for b in range(n) if b not in inside]
        for b in inside:
            bsnd[b] = acc[idx[o_ulast + BAND + b]].astype(jnp.bfloat16).reshape(bsnd.shape[1:])
            bwd_copy(b).start()
        for side, there in enumerate((has_right, has_left)):
            @pl.when(there)
            def _(side=side):
                rim_copy(side).wait_recv()
        for b in border:
            total = acc[idx[o_ulast + BAND + b]].reshape(bsnd.shape[1:])
            if b < BAND:
                total = total + rim_rcv[1, b].astype(jnp.float32)
            if b >= n - BAND:
                total = total + rim_rcv[0, b - (n - BAND)].astype(jnp.float32)
            bsnd[b] = total.astype(jnp.bfloat16)
            bwd_copy(b).start()

    for b in range(n):
        down_copy(b).wait()
        up_copy(b).wait()

        @pl.when(has_next)
        def _(b=b):
            fwd_copy(b).wait_send()

        @pl.when(has_prev)
        def _(b=b):
            bwd_copy(b).wait_send()
    for side, there in enumerate((has_left, has_right)):
        @pl.when(has_next & there)
        def _(side=side):
            halo_copy(side).wait_send()

        @pl.when(has_prev & there)
        def _(side=side):
            rim_copy(side).wait_send()


def on_device(source, tile_data, tile_rows, tile_cols, tile_count):
    layers, groups = lax.axis_size("layer"), lax.axis_size("blk")
    slots, tile = tile_data.shape[1], tile_data.shape[3]
    _, parts, half, length = source.shape
    n = length // tile
    idx, offsets = plan(tile_rows[0], tile_cols[0], tile_count[0, 0], lax.axis_index("blk") * n, n)
    block = (parts, half, tile)
    bf16 = jnp.bfloat16
    dma = pltpu.SemaphoreType.DMA
    shape = jax.ShapeDtypeStruct((parts, half, length), bf16)
    down, up = pl.pallas_call(
        functools.partial(kernel, layers, groups, n, slots, offsets),
        out_shape=(shape, shape),
        in_specs=[
            pl.BlockSpec(memory_space=pltpu.SMEM),
            pl.BlockSpec(memory_space=pl.ANY),
            pl.BlockSpec(memory_space=pl.ANY),
        ],
        out_specs=(pl.BlockSpec(memory_space=pl.ANY), pl.BlockSpec(memory_space=pl.ANY)),
        scratch_shapes=[
            pltpu.VMEM((slots, 2, tile, tile), bf16),
            pltpu.VMEM((slots + 1, parts * half, tile), jnp.float32),
            pltpu.VMEM((n,) + block, bf16),
            pltpu.VMEM((n + 2 * BAND,) + block, bf16),
            pltpu.VMEM((n,) + block, bf16),
            pltpu.VMEM((n,) + block, bf16),
            pltpu.VMEM((n,) + block, bf16),
            pltpu.VMEM((n,) + block, bf16),
            pltpu.VMEM((n,) + block, bf16),
            pltpu.VMEM((2, BAND) + block, bf16),
            pltpu.VMEM((2, BAND) + block, bf16),
            dma((slots,)),
            dma((n,)),
            dma((2, n)),
            dma((n,)),
            dma((n,)),
            dma((n,)),
            dma((n,)),
            dma((2,)),
            dma((2,)),
            dma((2,)),
            dma((2,)),
        ],
        compiler_params=pltpu.CompilerParams(
            collective_id=0, has_side_effects=True, vmem_limit_bytes=62 * 1024 * 1024
        ),
    )(idx, source[0], tile_data[0])
    return (down[None], up[None])


def solution(mesh):
    in_specs = (
        P("layer", None, None, "blk"),
        P("layer", "blk", None, None, None),
        P("layer", "blk"),
        P("layer", "blk"),
        P("layer", "blk"),
    )
    out_specs = (P("layer", None, None, "blk"), P("layer", None, None, "blk"))
    return jax.shard_map(
        on_device, mesh=mesh, in_specs=in_specs, out_specs=out_specs, check_vma=False
    )
```

```python
import functools

import jax
import jax.numpy as jnp
from jax import lax
from jax.experimental import pallas as pl
from jax.experimental.pallas import tpu as pltpu
from jax.sharding import PartitionSpec as P

BAND = 2
MESH = pl.DeviceIdType.MESH


SPAN = 2 * BAND + 1
RIMS = BAND * (BAND + 1)
CHUNK = 2 * BAND


def down_block(p, n):
    return (p + n - BAND) % n


def up_block(p, n):
    return (p + n // 2) % n


def sorted_by(key, values):
    slots = key.shape[0]
    rank = jnp.sum(key[None, :] < key[:, None], axis=1).astype(jnp.int32)
    place = rank[None, :] == jnp.arange(slots)[:, None]
    return rank, jnp.sum(jnp.where(place[None], values[:, None, :], 0), axis=2)


def plan(rows, cols, count, first_block, n, rest):
    slots = rows.shape[0]
    ids = jnp.arange(slots, dtype=jnp.int32)
    r = rows - first_block
    c = cols - first_block
    live = ids < count
    diag = live & (c == r)
    left, right = c < 0, c >= n
    rim = live & (left | right)
    big = n * slots
    key = jnp.where(live, ((r + BAND) % n) * slots, big) + ids
    key = jnp.where(diag, key + 2 * big, key)
    rank, (d_ord, d_col) = sorted_by(key, jnp.stack([ids, c + BAND]))
    d_pos = jnp.where(diag, r, n + rank)
    key = jnp.where(live, ((c + n - n // 2) % n) * slots, big) + ids
    key = jnp.where(diag | rim, key + 2 * big, key)
    rank, (u_ord, u_row) = sorted_by(key, jnp.stack([ids, r]))
    rim_at = jnp.where(left, r + c + BAND, RIMS // 2 + r + BAND - n + c - n)
    u_pos = jnp.where(diag, r, n + jnp.where(rim, rim_at, RIMS + rank))
    zero = max(slots, n + RIMS + rest)
    place = r * SPAN + c - r + BAND
    match = live[:, None] & (place[:, None] == jnp.arange(n * SPAN)[None, :])
    values = jnp.stack([ids, d_pos - zero, u_pos - zero])
    table, d_at, u_at = jnp.sum(jnp.where(match[None], values[:, :, None], 0), axis=1)
    parts = [table, d_at + zero, u_at + zero, d_ord, d_col, u_ord, u_row]
    offsets, at = [], 0
    for p in parts:
        offsets.append(at)
        at += p.shape[0]
    return jnp.concatenate([p.astype(jnp.int32) for p in parts]), offsets


def kernel(
    layers, groups, n, slots, rest, offsets,
    idx, source, tiles_hbm, down_out, up_out,
    tiles, acc, src, ext, up, inc, binc, snd, bsnd, rim_snd, rim_rcv,
    tile_sem, src_sem, out_sem, inc_send, inc_recv, binc_send, binc_recv,
    halo_send, halo_recv, rim_send, rim_recv,
):
    o_table, o_dat, o_uat, o_dord, o_dcol, o_uord, o_urow = offsets
    zero = acc.shape[0] - 1
    half, tile = src.shape[2], src.shape[3]
    layer = lax.axis_index("layer")
    blk = lax.axis_index("blk")
    has_prev, has_next = layer > 0, layer < layers - 1
    has_left, has_right = blk > 0, blk < groups - 1
    to_prev, to_next = (layer - 1, blk), (layer + 1, blk)
    to_left, to_right = (layer, blk - 1), (layer, blk + 1)
    partners = ((has_prev, to_prev), (has_next, to_next), (has_left, to_left), (has_right, to_right))

    def tile_copy(s):
        return pltpu.make_async_copy(tiles_hbm.at[s], tiles.at[s], tile_sem.at[s])

    def src_copy(b):
        return pltpu.make_async_copy(
            source.at[:, :, pl.ds(b * tile, tile)], src.at[b], src_sem.at[b]
        )

    def down_copy(b):
        return pltpu.make_async_copy(
            ext.at[BAND + b], down_out.at[:, :, pl.ds(b * tile, tile)], out_sem.at[0, b]
        )

    def up_copy(b):
        return pltpu.make_async_copy(
            up.at[b], up_out.at[:, :, pl.ds(b * tile, tile)], out_sem.at[1, b]
        )

    def fwd_copy(b):
        return pltpu.make_async_remote_copy(
            src_ref=snd.at[b], dst_ref=inc.at[b], send_sem=inc_send.at[b],
            recv_sem=inc_recv.at[b], device_id=to_next, device_id_type=MESH,
        )

    def bwd_copy(b):
        return pltpu.make_async_remote_copy(
            src_ref=bsnd.at[b], dst_ref=binc.at[b], send_sem=binc_send.at[b],
            recv_sem=binc_recv.at[b], device_id=to_prev, device_id_type=MESH,
        )

    def halo_copy(side):
        if side == 0:
            a, b, dev = ext.at[pl.ds(BAND, BAND)], ext.at[pl.ds(BAND + n, BAND)], to_left
        else:
            a, b, dev = ext.at[pl.ds(n, BAND)], ext.at[pl.ds(0, BAND)], to_right
        return pltpu.make_async_remote_copy(
            src_ref=a, dst_ref=b, send_sem=halo_send.at[side],
            recv_sem=halo_recv.at[side], device_id=dev, device_id_type=MESH,
        )

    def rim_copy(side):
        return pltpu.make_async_remote_copy(
            src_ref=rim_snd.at[side], dst_ref=rim_rcv.at[side], send_sem=rim_send.at[side],
            recv_sem=rim_recv.at[side], device_id=(to_left, to_right)[side], device_id_type=MESH,
        )

    for p in range(n):
        src_copy(down_block(p, n)).start()

    @pl.loop(0, slots)
    def _(s):
        tile_copy(s).start()

    barrier = pltpu.get_barrier_semaphore()
    for there, dev in partners:
        @pl.when(there)
        def _(dev=dev):
            pl.semaphore_signal(barrier, inc=1, device_id=dev, device_id_type=MESH)
    pl.semaphore_wait(barrier, sum(there.astype(jnp.int32) for there, _ in partners))

    def product(x, s, dim, write):
        x1 = x.reshape(2 * half, tile)
        x2 = jnp.concatenate([-x[1], x[0]], axis=0)
        numbers = (((1,), (dim,)), ((), ()))
        step = min(tile, 256)
        for j in range(0, tile, step):
            if dim == 1:
                real, imag = tiles[s, 0, j:j + step, :], tiles[s, 1, j:j + step, :]
            else:
                real, imag = tiles[s, 0, :, j:j + step], tiles[s, 1, :, j:j + step]
            y = lax.dot_general(x1, real, numbers, preferred_element_type=jnp.float32)
            y = y + lax.dot_general(x2, imag, numbers, preferred_element_type=jnp.float32)
            write(slice(j, j + step), y)

    @pl.when(jnp.logical_not(has_left))
    def _():
        ext[0:BAND] = jnp.zeros((BAND,) + ext.shape[1:], ext.dtype)
        rim_rcv[1] = jnp.zeros(rim_rcv.shape[1:], rim_rcv.dtype)

    @pl.when(jnp.logical_not(has_right))
    def _():
        ext[BAND + n:] = jnp.zeros((BAND,) + ext.shape[1:], ext.dtype)
        rim_rcv[0] = jnp.zeros(rim_rcv.shape[1:], rim_rcv.dtype)

    acc[zero] = jnp.zeros(acc.shape[1:], acc.dtype)

    def keep(place):
        def write(at, y):
            acc[place, :, at] = y

        return write

    def chunked(total, slot, after):
        @pl.loop(0, total // CHUNK)
        def _(p):
            for j in range(CHUNK):
                slot(p * CHUNK + j)
            after(p)

        for k in range(total // CHUNK * CHUNK, total):
            slot(k)

    @pl.loop(0, slots)
    def _(s):
        tile_copy(s).wait()

    border = min(n, 2 * BAND)

    def down_arrival(p):
        b = down_block(p, n)
        src_copy(b).wait()

        @pl.when(has_prev)
        def _():
            fwd_copy(b).wait_recv()
            total = src[b].astype(jnp.float32) + inc[b].astype(jnp.float32)
            ext[BAND + b] = total.astype(jnp.bfloat16)

        @pl.when(jnp.logical_not(has_prev))
        def _():
            ext[BAND + b] = src[b]

        down_copy(b).start()

    def down_diagonal(p):
        b = down_block(p, n)
        product(ext[BAND + b], idx[o_table + b * SPAN + BAND], 1, keep(b))

    pl.loop(0, border)(down_arrival)
    for side, there in enumerate((has_left, has_right)):
        @pl.when(has_next & there)
        def _(side=side):
            halo_copy(side).start()

    @pl.when(has_next)
    def _():
        pl.loop(0, border)(down_diagonal)

    @pl.loop(border, n)
    def _(p):
        down_arrival(p)

        @pl.when(has_next)
        def _():
            down_diagonal(p)

    @pl.when(has_next)
    def _():
        for side, there in enumerate((has_right, has_left)):
            @pl.when(there)
            def _(side=side):
                halo_copy(side).wait_recv()

        def slot(k):
            product(ext[idx[o_dcol + k]], idx[o_dord + k], 1, keep(n + k))

        def send(p):
            b = down_block(p, n)
            total = acc[b]
            for d in range(SPAN):
                if d != BAND:
                    total = total + acc[idx[o_dat + b * SPAN + d]]
            snd[b] = total.astype(jnp.bfloat16).reshape(snd.shape[1:])
            fwd_copy(b).start()

        chunked(slots - n, slot, send)
        pl.loop((slots - n) // CHUNK, n)(send)

    early = max(0, n - BAND - n // 2)

    def up_arrival(p):
        b = up_block(p, n)

        @pl.when(has_next)
        def _():
            bwd_copy(b).wait_recv()
            total = ext[BAND + b].astype(jnp.float32) + binc[b].astype(jnp.float32)
            up[b] = total.astype(jnp.bfloat16)

        @pl.when(jnp.logical_not(has_next))
        def _():
            up[b] = ext[BAND + b]

        up_copy(b).start()

        @pl.when(has_prev)
        def _():
            product(up[b], idx[o_table + b * SPAN + BAND], 0, keep(b))

    pl.loop(0, early + border)(up_arrival)

    @pl.when(has_prev)
    def _():
        @pl.loop(0, RIMS // 2)
        def _(j):
            low, high = j // 2, n - BAND + (j + 1) // 2
            product(up[low], idx[o_table + low * SPAN + j % 2], 0, keep(n + j))
            product(
                up[high], idx[o_table + high * SPAN + SPAN - 1 - j % 2], 0,
                keep(n + RIMS // 2 + j),
            )

        for side, there in enumerate((has_left, has_right)):
            for b in range(BAND):
                c = b - BAND if side == 0 else n + b
                near = [r for r in range(n) if abs(c - r) <= BAND]
                total = sum(acc[idx[o_uat + r * SPAN + c - r + BAND]] for r in near)
                rim_snd[side, b] = total.astype(jnp.bfloat16).reshape(rim_snd.shape[2:])

            @pl.when(there)
            def _(side=side):
                rim_copy(side).start()

    pl.loop(early + border, n)(up_arrival)

    @pl.when(has_prev)
    def _():
        def slot(k):
            product(up[idx[o_urow + k]], idx[o_uord + k], 0, keep(n + RIMS + k))

        def summed(b):
            total = acc[b]
            for r in range(-BAND, SPAN - BAND):
                if r != 0:
                    at = (b + r) * SPAN - r + BAND
                    inside = (b + r >= 0) & (b + r < n)
                    place = idx[o_uat + jnp.clip(at, 0, n * SPAN - 1)]
                    total = total + acc[jnp.where(inside, place, zero)]
            return total.reshape(bsnd.shape[1:])

        def send_inside(p):
            b = up_block(p, n)
            bsnd[b] = summed(b).astype(jnp.bfloat16)
            bwd_copy(b).start()

        def after(p):
            @pl.when(p < early)
            def _():
                send_inside(p)

        chunked(rest, slot, after)
        pl.loop(min(early, rest // CHUNK), early)(send_inside)
        for side, there in enumerate((has_right, has_left)):
            @pl.when(there)
            def _(side=side):
                rim_copy(side).wait_recv()
        for p in range(early, early + border):
            b = up_block(p, n)
            total = summed(b)
            if b < BAND:
                total = total + rim_rcv[1, b].astype(jnp.float32)
            if b >= n - BAND:
                total = total + rim_rcv[0, b - (n - BAND)].astype(jnp.float32)
            bsnd[b] = total.astype(jnp.bfloat16)
            bwd_copy(b).start()
        pl.loop(early + border, n)(send_inside)

    for b in range(n):
        down_copy(b).wait()
        up_copy(b).wait()

        @pl.when(has_next)
        def _(b=b):
            fwd_copy(b).wait_send()

        @pl.when(has_prev)
        def _(b=b):
            bwd_copy(b).wait_send()
    for side, there in enumerate((has_left, has_right)):
        @pl.when(has_next & there)
        def _(side=side):
            halo_copy(side).wait_send()

        @pl.when(has_prev & there)
        def _(side=side):
            rim_copy(side).wait_send()


def on_device(source, tile_data, tile_rows, tile_cols, tile_count):
    layers, groups = lax.axis_size("layer"), lax.axis_size("blk")
    slots, tile = tile_data.shape[1], tile_data.shape[3]
    _, parts, half, length = source.shape
    n = length // tile
    rest = slots - n - min(1, groups - 1)
    first_block = lax.axis_index("blk") * n
    idx, offsets = plan(tile_rows[0], tile_cols[0], tile_count[0, 0], first_block, n, rest)
    block = (parts, half, tile)
    bf16 = jnp.bfloat16
    dma = pltpu.SemaphoreType.DMA
    shape = jax.ShapeDtypeStruct((parts, half, length), bf16)
    down, up = pl.pallas_call(
        functools.partial(kernel, layers, groups, n, slots, rest, offsets),
        out_shape=(shape, shape),
        in_specs=[
            pl.BlockSpec(memory_space=pltpu.SMEM),
            pl.BlockSpec(memory_space=pl.ANY),
            pl.BlockSpec(memory_space=pl.ANY),
        ],
        out_specs=(pl.BlockSpec(memory_space=pl.ANY), pl.BlockSpec(memory_space=pl.ANY)),
        scratch_shapes=[
            pltpu.VMEM((slots, 2, tile, tile), bf16),
            pltpu.VMEM((max(slots, n + RIMS + rest) + 1, parts * half, tile), jnp.float32),
            pltpu.VMEM((n,) + block, bf16),
            pltpu.VMEM((n + 2 * BAND,) + block, bf16),
            pltpu.VMEM((n,) + block, bf16),
            pltpu.VMEM((n,) + block, bf16),
            pltpu.VMEM((n,) + block, bf16),
            pltpu.VMEM((n,) + block, bf16),
            pltpu.VMEM((n,) + block, bf16),
            pltpu.VMEM((2, BAND) + block, bf16),
            pltpu.VMEM((2, BAND) + block, bf16),
            dma((slots,)),
            dma((n,)),
            dma((2, n)),
            dma((n,)),
            dma((n,)),
            dma((n,)),
            dma((n,)),
            dma((2,)),
            dma((2,)),
            dma((2,)),
            dma((2,)),
        ],
        compiler_params=pltpu.CompilerParams(
            collective_id=0, has_side_effects=True, vmem_limit_bytes=62 * 1024 * 1024
        ),
    )(idx, source[0], tile_data[0])
    return (down[None], up[None])


def solution(mesh):
    in_specs = (
        P("layer", None, None, "blk"),
        P("layer", "blk", None, None, None),
        P("layer", "blk"),
        P("layer", "blk"),
        P("layer", "blk"),
    )
    out_specs = (P("layer", None, None, "blk"), P("layer", None, None, "blk"))
    return jax.shard_map(
        on_device, mesh=mesh, in_specs=in_specs, out_specs=out_specs, check_vma=False
    )
```

```python
import functools

import jax
import jax.numpy as jnp
from jax import lax
from jax.experimental import pallas as pl
from jax.experimental.pallas import tpu as pltpu
from jax.sharding import PartitionSpec as P

BAND = 2
MESH = pl.DeviceIdType.MESH


SPAN = 2 * BAND + 1
RIMS = BAND * (BAND + 1)
CHUNK = 2 * BAND


def down_block(p, n):
    return (p + n - BAND) % n


def up_block(p, n):
    return (p + n // 2) % n


def sorted_by(key, values):
    slots = key.shape[0]
    rank = jnp.sum(key[None, :] < key[:, None], axis=1).astype(jnp.int32)
    place = rank[None, :] == jnp.arange(slots)[:, None]
    return rank, jnp.sum(jnp.where(place[None], values[:, None, :], 0), axis=2)


def plan(rows, cols, count, first_block, n, rest):
    slots = rows.shape[0]
    ids = jnp.arange(slots, dtype=jnp.int32)
    r = rows - first_block
    c = cols - first_block
    live = ids < count
    diag = live & (c == r)
    left, right = c < 0, c >= n
    rim = live & (left | right)
    big = n * slots
    key = jnp.where(live, ((r + BAND) % n) * slots, big) + ids
    key = jnp.where(diag, key + 2 * big, key)
    rank, (d_ord, d_col) = sorted_by(key, jnp.stack([ids, c + BAND]))
    d_pos = jnp.where(diag, r, n + rank)
    key = jnp.where(live, ((c + n - n // 2) % n) * slots, big) + ids
    key = jnp.where(diag | rim, key + 2 * big, key)
    rank, (u_ord, u_row) = sorted_by(key, jnp.stack([ids, r]))
    rim_at = jnp.where(left, r + c + BAND, RIMS // 2 + r + BAND - n + c - n)
    u_pos = jnp.where(diag, r, n + jnp.where(rim, rim_at, RIMS + rank))
    zero = max(slots, n + RIMS + rest)
    place = r * SPAN + c - r + BAND
    match = live[:, None] & (place[:, None] == jnp.arange(n * SPAN)[None, :])
    values = jnp.stack([ids, d_pos - zero, u_pos - zero])
    table, d_at, u_at = jnp.sum(jnp.where(match[None], values[:, :, None], 0), axis=1)
    parts = [table, d_at + zero, u_at + zero, d_ord, d_col, u_ord, u_row]
    offsets, at = [], 0
    for p in parts:
        offsets.append(at)
        at += p.shape[0]
    return jnp.concatenate([p.astype(jnp.int32) for p in parts]), offsets


def kernel(
    layers, groups, n, slots, rest, offsets,
    idx, source, tiles_hbm, down_out, up_out,
    tiles, acc, src, ext, up, inc, binc, snd, bsnd, rim_snd, rim_rcv,
    tile_sem, src_sem, out_sem, inc_send, inc_recv, binc_send, binc_recv,
    halo_send, halo_recv, rim_send, rim_recv,
):
    o_table, o_dat, o_uat, o_dord, o_dcol, o_uord, o_urow = offsets
    zero = acc.shape[0] - 1
    half, tile = src.shape[2], src.shape[3]
    layer = lax.axis_index("layer")
    blk = lax.axis_index("blk")
    has_prev, has_next = layer > 0, layer < layers - 1
    has_left, has_right = blk > 0, blk < groups - 1
    to_prev, to_next = (layer - 1, blk), (layer + 1, blk)
    to_left, to_right = (layer, blk - 1), (layer, blk + 1)
    partners = ((has_prev, to_prev), (has_next, to_next), (has_left, to_left), (has_right, to_right))

    def tile_copy(s):
        return pltpu.make_async_copy(tiles_hbm.at[s], tiles.at[s], tile_sem.at[s])

    def src_copy(b):
        return pltpu.make_async_copy(
            source.at[:, :, pl.ds(b * tile, tile)], src.at[b], src_sem.at[b]
        )

    def down_copy(b):
        return pltpu.make_async_copy(
            ext.at[BAND + b], down_out.at[:, :, pl.ds(b * tile, tile)], out_sem.at[0, b]
        )

    def up_copy(b):
        return pltpu.make_async_copy(
            up.at[b], up_out.at[:, :, pl.ds(b * tile, tile)], out_sem.at[1, b]
        )

    def fwd_copy(b):
        return pltpu.make_async_remote_copy(
            src_ref=snd.at[b], dst_ref=inc.at[b], send_sem=inc_send.at[b],
            recv_sem=inc_recv.at[b], device_id=to_next, device_id_type=MESH,
        )

    def bwd_copy(b):
        return pltpu.make_async_remote_copy(
            src_ref=bsnd.at[b], dst_ref=binc.at[b], send_sem=binc_send.at[b],
            recv_sem=binc_recv.at[b], device_id=to_prev, device_id_type=MESH,
        )

    def halo_copy(side, i):
        near, far, dev = (BAND + i, BAND + n + i, to_left) if side == 0 else (n + i, i, to_right)
        return pltpu.make_async_remote_copy(
            src_ref=ext.at[near], dst_ref=ext.at[far], send_sem=halo_send.at[side, i],
            recv_sem=halo_recv.at[side, i], device_id=dev, device_id_type=MESH,
        )

    def rim_copy(side, i):
        return pltpu.make_async_remote_copy(
            src_ref=rim_snd.at[side, i], dst_ref=rim_rcv.at[side, i],
            send_sem=rim_send.at[side, i], recv_sem=rim_recv.at[side, i],
            device_id=(to_left, to_right)[side], device_id_type=MESH,
        )

    for p in range(n):
        src_copy(down_block(p, n)).start()

    @pl.loop(0, slots)
    def _(s):
        tile_copy(s).start()

    barrier = pltpu.get_barrier_semaphore()
    for there, dev in partners:
        @pl.when(there)
        def _(dev=dev):
            pl.semaphore_signal(barrier, inc=1, device_id=dev, device_id_type=MESH)
    pl.semaphore_wait(barrier, sum(there.astype(jnp.int32) for there, _ in partners))

    def product(x, s, dim, write):
        both = jnp.concatenate(
            [x.reshape(2 * half, tile), jnp.concatenate([-x[1], x[0]], axis=0)], axis=1
        )
        if dim == 1:
            matrix = jnp.concatenate([tiles[s, 0], tiles[s, 1]], axis=1)
        else:
            matrix = tiles[s].reshape(2 * tile, tile)
        numbers = (((1,), (dim,)), ((), ()))
        y = lax.dot_general(both, matrix, numbers, preferred_element_type=jnp.float32)
        write(slice(None), y)

    @pl.when(jnp.logical_not(has_left))
    def _():
        ext[0:BAND] = jnp.zeros((BAND,) + ext.shape[1:], ext.dtype)
        rim_rcv[1] = jnp.zeros(rim_rcv.shape[1:], rim_rcv.dtype)

    @pl.when(jnp.logical_not(has_right))
    def _():
        ext[BAND + n:] = jnp.zeros((BAND,) + ext.shape[1:], ext.dtype)
        rim_rcv[0] = jnp.zeros(rim_rcv.shape[1:], rim_rcv.dtype)

    acc[zero] = jnp.zeros(acc.shape[1:], acc.dtype)

    def keep(place):
        def write(at, y):
            acc[place, :, at] = y

        return write

    def chunked(total, slot, after):
        @pl.loop(0, total // CHUNK)
        def _(p):
            for j in range(CHUNK):
                slot(p * CHUNK + j)
            after(p)

        for k in range(total // CHUNK * CHUNK, total):
            slot(k)

    border = min(n, 2 * BAND)

    def down_arrival(p):
        b = down_block(p, n)
        src_copy(b).wait()

        @pl.when(has_prev)
        def _():
            fwd_copy(b).wait_recv()
            total = src[b].astype(jnp.float32) + inc[b].astype(jnp.float32)
            ext[BAND + b] = total.astype(jnp.bfloat16)

        @pl.when(jnp.logical_not(has_prev))
        def _():
            ext[BAND + b] = src[b]

        down_copy(b).start()

    def down_diagonal(p):
        b = down_block(p, n)
        product(ext[BAND + b], idx[o_table + b * SPAN + BAND], 1, keep(b))

    @pl.loop(0, border)
    def _(p):
        b = down_block(p, n)
        down_arrival(p)

        @pl.when(has_next & has_right & (b >= n - BAND))
        def _():
            halo_copy(1, b - (n - BAND)).start()

        @pl.when(has_next & has_left & (b < BAND))
        def _():
            halo_copy(0, b).start()

    @pl.loop(0, slots)
    def _(s):
        tile_copy(s).wait()

    @pl.when(has_next)
    def _():
        pl.loop(0, border)(down_diagonal)

    @pl.loop(border, n)
    def _(p):
        down_arrival(p)

        @pl.when(has_next)
        def _():
            down_diagonal(p)

    @pl.when(has_next)
    def _():
        for side, there in enumerate((has_right, has_left)):
            @pl.when(there)
            def _(side=side):
                for i in range(BAND):
                    halo_copy(side, i).wait_recv()

        def slot(k):
            product(ext[idx[o_dcol + k]], idx[o_dord + k], 1, keep(n + k))

        def send(p):
            b = down_block(p, n)
            total = acc[b]
            for d in range(SPAN):
                if d != BAND:
                    total = total + acc[idx[o_dat + b * SPAN + d]]
            snd[b] = total.astype(jnp.bfloat16).reshape(snd.shape[1:])
            fwd_copy(b).start()

        chunked(slots - n, slot, send)
        pl.loop((slots - n) // CHUNK, n)(send)

    early = max(0, n - BAND - n // 2)

    def up_diagonal(b):
        product(up[b], idx[o_table + b * SPAN + BAND], 0, keep(b))

    def up_arrival(p):
        b = up_block(p, n)

        @pl.when(has_next)
        def _():
            bwd_copy(b).wait_recv()
            total = ext[BAND + b].astype(jnp.float32) + binc[b].astype(jnp.float32)
            up[b] = total.astype(jnp.bfloat16)

        @pl.when(jnp.logical_not(has_next))
        def _():
            up[b] = ext[BAND + b]

        up_copy(b).start()

        @pl.when(has_prev & has_next)
        def _():
            up_diagonal(b)

    pl.loop(0, early + border)(up_arrival)

    @pl.when(has_prev)
    def _():
        def rim_pair(j):
            low, high = j // 2, n - BAND + (BAND + 1 - j) // 2
            product(up[low], idx[o_table + low * SPAN + j % 2], 0, keep(n + j))
            product(
                up[high], idx[o_table + high * SPAN + SPAN - 1 - j % 2], 0,
                keep(n + RIMS - 1 - j),
            )

        def rim_start(side, b):
            c = b - BAND if side == 0 else n + b
            near = [r for r in range(n) if abs(c - r) <= BAND]
            total = sum(acc[idx[o_uat + r * SPAN + c - r + BAND]] for r in near)
            rim_snd[side, b] = total.astype(jnp.bfloat16).reshape(rim_snd.shape[2:])

            @pl.when((has_left, has_right)[side])
            def _():
                rim_copy(side, b).start()

        rim_pair(0)
        rim_start(0, 0)
        rim_start(1, 1)
        pl.loop(1, RIMS // 2)(rim_pair)
        rim_start(0, 1)
        rim_start(1, 0)

    pl.loop(early + border, n)(up_arrival)

    @pl.when(has_prev & jnp.logical_not(has_next))
    def _():
        pl.loop(0, n)(up_diagonal)

    @pl.when(has_prev)
    def _():
        def slot(k):
            product(up[idx[o_urow + k]], idx[o_uord + k], 0, keep(n + RIMS + k))

        def summed(b):
            total = acc[b]
            for r in range(-BAND, SPAN - BAND):
                if r != 0:
                    at = (b + r) * SPAN - r + BAND
                    inside = (b + r >= 0) & (b + r < n)
                    place = idx[o_uat + jnp.clip(at, 0, n * SPAN - 1)]
                    total = total + acc[jnp.where(inside, place, zero)]
            return total.reshape(bsnd.shape[1:])

        def send_inside(p):
            b = up_block(p, n)
            bsnd[b] = summed(b).astype(jnp.bfloat16)
            bwd_copy(b).start()

        def after(p):
            @pl.when(p < early)
            def _():
                send_inside(p)

        chunked(rest, slot, after)
        pl.loop(min(early, rest // CHUNK), early)(send_inside)
        for side, there in enumerate((has_right, has_left)):
            @pl.when(there)
            def _(side=side):
                for i in range(BAND):
                    rim_copy(side, i).wait_recv()
        for p in range(early, early + border):
            b = up_block(p, n)
            total = summed(b)
            if b < BAND:
                total = total + rim_rcv[1, b].astype(jnp.float32)
            if b >= n - BAND:
                total = total + rim_rcv[0, b - (n - BAND)].astype(jnp.float32)
            bsnd[b] = total.astype(jnp.bfloat16)
            bwd_copy(b).start()
        pl.loop(early + border, n)(send_inside)

    for b in range(n):
        down_copy(b).wait()
        up_copy(b).wait()

        @pl.when(has_next)
        def _(b=b):
            fwd_copy(b).wait_send()

        @pl.when(has_prev)
        def _(b=b):
            bwd_copy(b).wait_send()
    for side, there in enumerate((has_left, has_right)):
        @pl.when(has_next & there)
        def _(side=side):
            for i in range(BAND):
                halo_copy(side, i).wait_send()

        @pl.when(has_prev & there)
        def _(side=side):
            for i in range(BAND):
                rim_copy(side, i).wait_send()


def on_device(source, tile_data, tile_rows, tile_cols, tile_count):
    layers, groups = lax.axis_size("layer"), lax.axis_size("blk")
    slots, tile = tile_data.shape[1], tile_data.shape[3]
    _, parts, half, length = source.shape
    n = length // tile
    rest = slots - n - min(1, groups - 1)
    first_block = lax.axis_index("blk") * n
    idx, offsets = plan(tile_rows[0], tile_cols[0], tile_count[0, 0], first_block, n, rest)
    block = (parts, half, tile)
    bf16 = jnp.bfloat16
    dma = pltpu.SemaphoreType.DMA
    shape = jax.ShapeDtypeStruct((parts, half, length), bf16)
    down, up = pl.pallas_call(
        functools.partial(kernel, layers, groups, n, slots, rest, offsets),
        out_shape=(shape, shape),
        in_specs=[
            pl.BlockSpec(memory_space=pltpu.SMEM),
            pl.BlockSpec(memory_space=pl.ANY),
            pl.BlockSpec(memory_space=pl.ANY),
        ],
        out_specs=(pl.BlockSpec(memory_space=pl.ANY), pl.BlockSpec(memory_space=pl.ANY)),
        scratch_shapes=[
            pltpu.VMEM((slots, 2, tile, tile), bf16),
            pltpu.VMEM((max(slots, n + RIMS + rest) + 1, parts * half, tile), jnp.float32),
            pltpu.VMEM((n,) + block, bf16),
            pltpu.VMEM((n + 2 * BAND,) + block, bf16),
            pltpu.VMEM((n,) + block, bf16),
            pltpu.VMEM((n,) + block, bf16),
            pltpu.VMEM((n,) + block, bf16),
            pltpu.VMEM((n,) + block, bf16),
            pltpu.VMEM((n,) + block, bf16),
            pltpu.VMEM((2, BAND) + block, bf16),
            pltpu.VMEM((2, BAND) + block, bf16),
            dma((slots,)),
            dma((n,)),
            dma((2, n)),
            dma((n,)),
            dma((n,)),
            dma((n,)),
            dma((n,)),
            dma((2, BAND)),
            dma((2, BAND)),
            dma((2, BAND)),
            dma((2, BAND)),
        ],
        compiler_params=pltpu.CompilerParams(
            collective_id=0, has_side_effects=True, vmem_limit_bytes=62 * 1024 * 1024
        ),
    )(idx, source[0], tile_data[0])
    return (down[None], up[None])


def solution(mesh):
    in_specs = (
        P("layer", None, None, "blk"),
        P("layer", "blk", None, None, None),
        P("layer", "blk"),
        P("layer", "blk"),
        P("layer", "blk"),
    )
    out_specs = (P("layer", None, None, "blk"), P("layer", None, None, "blk"))
    return jax.shard_map(
        on_device, mesh=mesh, in_specs=in_specs, out_specs=out_specs, check_vma=False
    )
```

```python
import functools

import jax
import jax.numpy as jnp
from jax import lax
from jax.experimental import pallas as pl
from jax.experimental.pallas import tpu as pltpu
from jax.sharding import PartitionSpec as P

BAND = 2
MESH = pl.DeviceIdType.MESH


SPAN = 2 * BAND + 1
RIMS = BAND * (BAND + 1)
CHUNK = 2 * BAND


def down_block(p, n):
    return (p + n - BAND) % n


def up_early(n):
    return max(0, n - 2 * BAND - 1)


def up_block(p, n):
    return (p + n - BAND - up_early(n)) % n


def sorted_by(key, values):
    slots = key.shape[0]
    rank = jnp.sum(key[None, :] < key[:, None], axis=1).astype(jnp.int32)
    place = rank[None, :] == jnp.arange(slots)[:, None]
    return rank, jnp.sum(jnp.where(place[None], values[:, None, :], 0), axis=2)


def plan(rows, cols, count, first_block, n, rest):
    slots = rows.shape[0]
    ids = jnp.arange(slots, dtype=jnp.int32)
    r = rows - first_block
    c = cols - first_block
    live = ids < count
    diag = live & (c == r)
    left, right = c < 0, c >= n
    rim = live & (left | right)
    big = n * slots
    key = jnp.where(live, ((r + BAND) % n) * slots, big) + ids
    key = jnp.where(diag, key + 2 * big, key)
    rank, (d_ord, d_col) = sorted_by(key, jnp.stack([ids, c + BAND]))
    d_pos = jnp.where(diag, r, n + rank)
    key = jnp.where(live, ((c + BAND + up_early(n)) % n) * slots, big) + ids
    key = jnp.where(diag | rim, key + 2 * big, key)
    rank, (u_ord, u_row) = sorted_by(key, jnp.stack([ids, r]))
    rim_at = jnp.where(left, r + c + BAND, RIMS // 2 + r + BAND - n + c - n)
    u_pos = jnp.where(diag, r, n + jnp.where(rim, rim_at, RIMS + rank))
    zero = max(slots, n + RIMS + rest)
    place = r * SPAN + c - r + BAND
    match = live[:, None] & (place[:, None] == jnp.arange(n * SPAN)[None, :])
    values = jnp.stack([ids, d_pos - zero, u_pos - zero])
    table, d_at, u_at = jnp.sum(jnp.where(match[None], values[:, :, None], 0), axis=1)
    parts = [table, d_at + zero, u_at + zero, d_ord, d_col, u_ord, u_row]
    offsets, at = [], 0
    for p in parts:
        offsets.append(at)
        at += p.shape[0]
    return jnp.concatenate([p.astype(jnp.int32) for p in parts]), offsets


def kernel(
    layers, groups, n, slots, rest, offsets,
    idx, source, tiles_hbm, down_out, up_out,
    tiles, acc, src, ext, up, inc, binc, snd, bsnd, rim_snd, rim_rcv,
    tile_sem, src_sem, out_sem, inc_send, inc_recv, binc_send, binc_recv,
    halo_send, halo_recv, rim_send, rim_recv,
):
    o_table, o_dat, o_uat, o_dord, o_dcol, o_uord, o_urow = offsets
    zero = acc.shape[0] - 1
    half, tile = src.shape[2], src.shape[3]
    layer = lax.axis_index("layer")
    blk = lax.axis_index("blk")
    has_prev, has_next = layer > 0, layer < layers - 1
    has_left, has_right = blk > 0, blk < groups - 1
    to_prev, to_next = (layer - 1, blk), (layer + 1, blk)
    to_left, to_right = (layer, blk - 1), (layer, blk + 1)
    partners = ((has_prev, to_prev), (has_next, to_next), (has_left, to_left), (has_right, to_right))

    def tile_copy(s):
        return pltpu.make_async_copy(tiles_hbm.at[s], tiles.at[s], tile_sem.at[s])

    def src_copy(b):
        return pltpu.make_async_copy(
            source.at[:, :, pl.ds(b * tile, tile)], src.at[b], src_sem.at[b]
        )

    def down_copy(b):
        return pltpu.make_async_copy(
            ext.at[BAND + b], down_out.at[:, :, pl.ds(b * tile, tile)], out_sem.at[0, b]
        )

    def up_copy(b):
        return pltpu.make_async_copy(
            up.at[b], up_out.at[:, :, pl.ds(b * tile, tile)], out_sem.at[1, b]
        )

    def fwd_copy(b):
        return pltpu.make_async_remote_copy(
            src_ref=snd.at[b], dst_ref=inc.at[b], send_sem=inc_send.at[b],
            recv_sem=inc_recv.at[b], device_id=to_next, device_id_type=MESH,
        )

    def bwd_copy(b):
        return pltpu.make_async_remote_copy(
            src_ref=bsnd.at[b], dst_ref=binc.at[b], send_sem=binc_send.at[b],
            recv_sem=binc_recv.at[b], device_id=to_prev, device_id_type=MESH,
        )

    def halo_copy(side, i):
        near, far, dev = (BAND + i, BAND + n + i, to_left) if side == 0 else (n + i, i, to_right)
        return pltpu.make_async_remote_copy(
            src_ref=ext.at[near], dst_ref=ext.at[far], send_sem=halo_send.at[side, i],
            recv_sem=halo_recv.at[side, i], device_id=dev, device_id_type=MESH,
        )

    def rim_copy(side, i):
        return pltpu.make_async_remote_copy(
            src_ref=rim_snd.at[side, i], dst_ref=rim_rcv.at[side, i],
            send_sem=rim_send.at[side, i], recv_sem=rim_recv.at[side, i],
            device_id=(to_left, to_right)[side], device_id_type=MESH,
        )

    for p in range(n):
        src_copy(down_block(p, n)).start()

    @pl.loop(0, slots)
    def _(s):
        tile_copy(s).start()

    barrier = pltpu.get_barrier_semaphore()
    for there, dev in partners:
        @pl.when(there)
        def _(dev=dev):
            pl.semaphore_signal(barrier, inc=1, device_id=dev, device_id_type=MESH)
    pl.semaphore_wait(barrier, sum(there.astype(jnp.int32) for there, _ in partners))

    def product(x, s, dim, write):
        both = jnp.concatenate(
            [x.reshape(2 * half, tile), jnp.concatenate([-x[1], x[0]], axis=0)], axis=1
        )
        if dim == 1:
            matrix = jnp.concatenate([tiles[s, 0], tiles[s, 1]], axis=1)
        else:
            matrix = tiles[s].reshape(2 * tile, tile)
        numbers = (((1,), (dim,)), ((), ()))
        y = lax.dot_general(both, matrix, numbers, preferred_element_type=jnp.float32)
        write(slice(None), y)

    @pl.when(jnp.logical_not(has_left))
    def _():
        ext[0:BAND] = jnp.zeros((BAND,) + ext.shape[1:], ext.dtype)
        rim_rcv[1] = jnp.zeros(rim_rcv.shape[1:], rim_rcv.dtype)

    @pl.when(jnp.logical_not(has_right))
    def _():
        ext[BAND + n:] = jnp.zeros((BAND,) + ext.shape[1:], ext.dtype)
        rim_rcv[0] = jnp.zeros(rim_rcv.shape[1:], rim_rcv.dtype)

    acc[zero] = jnp.zeros(acc.shape[1:], acc.dtype)

    def keep(place):
        def write(at, y):
            acc[place, :, at] = y

        return write

    def chunked(total, slot, after, first=0):
        @pl.loop(first, total // CHUNK)
        def _(p):
            for j in range(CHUNK):
                slot(p * CHUNK + j)
            after(p)

        for k in range(total // CHUNK * CHUNK, total):
            slot(k)

    border = min(n, 2 * BAND)

    def down_arrival(p):
        b = down_block(p, n)
        src_copy(b).wait()

        @pl.when(has_prev)
        def _():
            fwd_copy(b).wait_recv()
            total = src[b].astype(jnp.float32) + inc[b].astype(jnp.float32)
            ext[BAND + b] = total.astype(jnp.bfloat16)

        @pl.when(jnp.logical_not(has_prev))
        def _():
            ext[BAND + b] = src[b]

        down_copy(b).start()

    def down_diagonal(p):
        b = down_block(p, n)
        product(ext[BAND + b], idx[o_table + b * SPAN + BAND], 1, keep(b))

    @pl.loop(0, border)
    def _(p):
        b = down_block(p, n)
        down_arrival(p)

        @pl.when(has_next & has_right & (b >= n - BAND))
        def _():
            halo_copy(1, b - (n - BAND)).start()

        @pl.when(has_next & has_left & (b < BAND))
        def _():
            halo_copy(0, b).start()

    @pl.loop(0, slots)
    def _(s):
        tile_copy(s).wait()

    @pl.when(has_next)
    def _():
        pl.loop(0, border)(down_diagonal)

    @pl.loop(border, n)
    def _(p):
        down_arrival(p)

        @pl.when(has_next)
        def _():
            down_diagonal(p)

    @pl.when(has_next)
    def _():
        for side, there in enumerate((has_right, has_left)):
            @pl.when(there)
            def _(side=side):
                for i in range(BAND):
                    halo_copy(side, i).wait_recv()

        def slot(k):
            product(ext[idx[o_dcol + k]], idx[o_dord + k], 1, keep(n + k))

        def send(p):
            b = down_block(p, n)
            total = acc[b]
            for d in range(SPAN):
                if d != BAND:
                    total = total + acc[idx[o_dat + b * SPAN + d]]
            snd[b] = total.astype(jnp.bfloat16).reshape(snd.shape[1:])
            fwd_copy(b).start()

        chunked(slots - n, slot, send)
        pl.loop((slots - n) // CHUNK, n)(send)

    early = up_early(n)

    def up_diagonal(b):
        product(up[b], idx[o_table + b * SPAN + BAND], 0, keep(b))

    def up_arrival(p):
        b = up_block(p, n)

        @pl.when(has_next)
        def _():
            bwd_copy(b).wait_recv()
            total = ext[BAND + b].astype(jnp.float32) + binc[b].astype(jnp.float32)
            up[b] = total.astype(jnp.bfloat16)

        @pl.when(jnp.logical_not(has_next))
        def _():
            up[b] = ext[BAND + b]

        up_copy(b).start()

        @pl.when(has_prev & has_next)
        def _():
            up_diagonal(b)

    pl.loop(0, early + border)(up_arrival)

    def rim_pair(j):
        low, high = j // 2, n - BAND + (BAND + 1 - j) // 2
        product(up[low], idx[o_table + low * SPAN + j % 2], 0, keep(n + j))
        product(
            up[high], idx[o_table + high * SPAN + SPAN - 1 - j % 2], 0,
            keep(n + RIMS - 1 - j),
        )

    def rim_start(side, b):
        c = b - BAND if side == 0 else n + b
        near = [r for r in range(n) if abs(c - r) <= BAND]
        total = sum(acc[idx[o_uat + r * SPAN + c - r + BAND]] for r in near)
        rim_snd[side, b] = total.astype(jnp.bfloat16).reshape(rim_snd.shape[2:])

        @pl.when((has_left, has_right)[side])
        def _():
            rim_copy(side, b).start()

    @pl.when(has_prev)
    def _():
        rim_pair(0)
        rim_start(0, 0)
        rim_start(1, 1)
    pl.loop(early + border, n)(up_arrival)

    @pl.when(has_prev & jnp.logical_not(has_next))
    def _():
        pl.loop(0, n)(up_diagonal)

    @pl.when(has_prev)
    def _():
        def slot(k):
            product(up[idx[o_urow + k]], idx[o_uord + k], 0, keep(n + RIMS + k))

        def summed(b):
            total = acc[b]
            for r in range(-BAND, SPAN - BAND):
                if r != 0:
                    at = (b + r) * SPAN - r + BAND
                    inside = (b + r >= 0) & (b + r < n)
                    place = idx[o_uat + jnp.clip(at, 0, n * SPAN - 1)]
                    total = total + acc[jnp.where(inside, place, zero)]
            return total.reshape(bsnd.shape[1:])

        def send_inside(p):
            b = up_block(p, n)
            bsnd[b] = summed(b).astype(jnp.bfloat16)
            bwd_copy(b).start()

        def after(p):
            @pl.when(p < early)
            def _():
                send_inside(p)

        first = min(1, rest // CHUNK)
        for k in range(first * CHUNK):
            slot(k)
        if first and early:
            send_inside(0)
        pl.loop(1, RIMS // 2)(rim_pair)
        rim_start(0, 1)
        rim_start(1, 0)
        chunked(rest, slot, after, first)
        pl.loop(min(early, rest // CHUNK), early)(send_inside)
        for side, there in enumerate((has_right, has_left)):
            @pl.when(there)
            def _(side=side):
                for i in range(BAND):
                    rim_copy(side, i).wait_recv()
        for p in range(early, early + border):
            b = up_block(p, n)
            total = summed(b)
            if b < BAND:
                total = total + rim_rcv[1, b].astype(jnp.float32)
            if b >= n - BAND:
                total = total + rim_rcv[0, b - (n - BAND)].astype(jnp.float32)
            bsnd[b] = total.astype(jnp.bfloat16)
            bwd_copy(b).start()
        pl.loop(early + border, n)(send_inside)

    for b in range(n):
        down_copy(b).wait()
        up_copy(b).wait()

        @pl.when(has_next)
        def _(b=b):
            fwd_copy(b).wait_send()

        @pl.when(has_prev)
        def _(b=b):
            bwd_copy(b).wait_send()
    for side, there in enumerate((has_left, has_right)):
        @pl.when(has_next & there)
        def _(side=side):
            for i in range(BAND):
                halo_copy(side, i).wait_send()

        @pl.when(has_prev & there)
        def _(side=side):
            for i in range(BAND):
                rim_copy(side, i).wait_send()


def hand_out(down_in, up_in, down_out, up_out, sem):
    copies = [
        pltpu.make_async_copy(a.at[h], b.at[h], sem.at[i, h])
        for i, (a, b) in enumerate(((down_in, down_out), (up_in, up_out)))
        for h in range(2)
    ]
    for copy in copies:
        copy.start()
    for copy in copies:
        copy.wait()


def on_device(source, tile_data, tile_rows, tile_cols, tile_count):
    layers, groups = lax.axis_size("layer"), lax.axis_size("blk")
    slots, tile = tile_data.shape[1], tile_data.shape[3]
    _, parts, half, length = source.shape
    n = length // tile
    rest = slots - n - min(1, groups - 1)
    first_block = lax.axis_index("blk") * n
    idx, offsets = plan(tile_rows[0], tile_cols[0], tile_count[0, 0], first_block, n, rest)
    block = (parts, half, tile)
    bf16 = jnp.bfloat16
    dma = pltpu.SemaphoreType.DMA
    shape = jax.ShapeDtypeStruct((parts, half, length), bf16)
    down, up = pl.pallas_call(
        functools.partial(kernel, layers, groups, n, slots, rest, offsets),
        out_shape=(shape, shape),
        in_specs=[
            pl.BlockSpec(memory_space=pltpu.SMEM),
            pl.BlockSpec(memory_space=pl.ANY),
            pl.BlockSpec(memory_space=pl.ANY),
        ],
        out_specs=(pl.BlockSpec(memory_space=pl.ANY), pl.BlockSpec(memory_space=pl.ANY)),
        scratch_shapes=[
            pltpu.VMEM((slots, 2, tile, tile), bf16),
            pltpu.VMEM((max(slots, n + RIMS + rest) + 1, parts * half, tile), jnp.float32),
            pltpu.VMEM((n,) + block, bf16),
            pltpu.VMEM((n + 2 * BAND,) + block, bf16),
            pltpu.VMEM((n,) + block, bf16),
            pltpu.VMEM((n,) + block, bf16),
            pltpu.VMEM((n,) + block, bf16),
            pltpu.VMEM((n,) + block, bf16),
            pltpu.VMEM((n,) + block, bf16),
            pltpu.VMEM((2, BAND) + block, bf16),
            pltpu.VMEM((2, BAND) + block, bf16),
            dma((slots,)),
            dma((n,)),
            dma((2, n)),
            dma((n,)),
            dma((n,)),
            dma((n,)),
            dma((n,)),
            dma((2, BAND)),
            dma((2, BAND)),
            dma((2, BAND)),
            dma((2, BAND)),
        ],
        compiler_params=pltpu.CompilerParams(
            collective_id=0, has_side_effects=True, vmem_limit_bytes=62 * 1024 * 1024
        ),
    )(idx, source[0], tile_data[0])
    down, up = pl.pallas_call(
        hand_out,
        out_shape=(shape, shape),
        in_specs=[pl.BlockSpec(memory_space=pl.ANY)] * 2,
        out_specs=(pl.BlockSpec(memory_space=pl.ANY),) * 2,
        scratch_shapes=[dma((2, 2))],
        compiler_params=pltpu.CompilerParams(vmem_limit_bytes=62 * 1024 * 1024),
    )(down, up)
    return (down[None], up[None])


def solution(mesh):
    in_specs = (
        P("layer", None, None, "blk"),
        P("layer", "blk", None, None, None),
        P("layer", "blk"),
        P("layer", "blk"),
        P("layer", "blk"),
    )
    out_specs = (P("layer", None, None, "blk"), P("layer", None, None, "blk"))
    return jax.shard_map(
        on_device, mesh=mesh, in_specs=in_specs, out_specs=out_specs, check_vma=False
    )
```

```python
import functools

import jax
import jax.numpy as jnp
from jax import lax
from jax.experimental import pallas as pl
from jax.experimental.pallas import tpu as pltpu
from jax.sharding import PartitionSpec as P

BAND = 2
MESH = pl.DeviceIdType.MESH


SPAN = 2 * BAND + 1
RIMS = BAND * (BAND + 1)
CHUNK = 2 * BAND


def down_block(p, n):
    return (p + n - BAND) % n


def up_early(n):
    return max(0, n - 2 * BAND - 1)


def up_block(p, n):
    return (p + n - BAND - up_early(n)) % n


def sorted_by(key, values):
    slots = key.shape[0]
    rank = jnp.sum(key[None, :] < key[:, None], axis=1).astype(jnp.int32)
    place = rank[None, :] == jnp.arange(slots)[:, None]
    return rank, jnp.sum(jnp.where(place[None], values[:, None, :], 0), axis=2)


def plan(rows, cols, count, first_block, n, rest):
    slots = rows.shape[0]
    ids = jnp.arange(slots, dtype=jnp.int32)
    r = rows - first_block
    c = cols - first_block
    live = ids < count
    diag = live & (c == r)
    left, right = c < 0, c >= n
    rim = live & (left | right)
    big = n * slots
    key = jnp.where(live, ((r + BAND) % n) * slots, big) + ids
    key = jnp.where(diag, key + 2 * big, key)
    rank, (d_ord, d_col) = sorted_by(key, jnp.stack([ids, c + BAND]))
    d_pos = jnp.where(diag, r, n + rank)
    key = jnp.where(live, ((c + BAND + up_early(n)) % n) * slots, big) + ids
    key = jnp.where(diag | rim, key + 2 * big, key)
    rank, (u_ord, u_row) = sorted_by(key, jnp.stack([ids, r]))
    rim_at = jnp.where(left, r + c + BAND, RIMS // 2 + r + BAND - n + c - n)
    u_pos = jnp.where(diag, r, n + jnp.where(rim, rim_at, RIMS + rank))
    zero = max(slots, n + RIMS + rest)
    place = r * SPAN + c - r + BAND
    match = live[:, None] & (place[:, None] == jnp.arange(n * SPAN)[None, :])
    values = jnp.stack([ids, d_pos - zero, u_pos - zero])
    table, d_at, u_at = jnp.sum(jnp.where(match[None], values[:, :, None], 0), axis=1)
    parts = [table, d_at + zero, u_at + zero, d_ord, d_col, u_ord, u_row]
    offsets, at = [], 0
    for p in parts:
        offsets.append(at)
        at += p.shape[0]
    return jnp.concatenate([p.astype(jnp.int32) for p in parts]), offsets


def kernel(
    layers, groups, n, slots, rest, offsets,
    idx, source, tiles_hbm, down_out, up_out,
    tiles, acc, src, ext, up, inc, binc, snd, bsnd, rim_snd, rim_rcv,
    tile_sem, src_sem, out_sem, inc_send, inc_recv, binc_send, binc_recv,
    halo_send, halo_recv, rim_send, rim_recv,
):
    o_table, o_dat, o_uat, o_dord, o_dcol, o_uord, o_urow = offsets
    zero = acc.shape[0] - 1
    half, tile = src.shape[2], src.shape[3]
    layer = lax.axis_index("layer")
    blk = lax.axis_index("blk")
    has_prev, has_next = layer > 0, layer < layers - 1
    has_left, has_right = blk > 0, blk < groups - 1
    to_prev, to_next = (layer - 1, blk), (layer + 1, blk)
    to_left, to_right = (layer, blk - 1), (layer, blk + 1)
    partners = ((has_prev, to_prev), (has_next, to_next), (has_left, to_left), (has_right, to_right))

    def tile_copy(s):
        return pltpu.make_async_copy(tiles_hbm.at[s], tiles.at[s], tile_sem.at[s])

    def src_copy(b):
        return pltpu.make_async_copy(
            source.at[:, :, pl.ds(b * tile, tile)], src.at[b], src_sem.at[b]
        )

    def down_copy(b):
        return pltpu.make_async_copy(
            ext.at[BAND + b], down_out.at[:, :, pl.ds(b * tile, tile)], out_sem.at[0, b]
        )

    def up_copy(b):
        return pltpu.make_async_copy(
            up.at[b], up_out.at[:, :, pl.ds(b * tile, tile)], out_sem.at[1, b]
        )

    def fwd_copy(b):
        return pltpu.make_async_remote_copy(
            src_ref=snd.at[b], dst_ref=inc.at[b], send_sem=inc_send.at[b],
            recv_sem=inc_recv.at[b], device_id=to_next, device_id_type=MESH,
        )

    def bwd_copy(b):
        return pltpu.make_async_remote_copy(
            src_ref=bsnd.at[b], dst_ref=binc.at[b], send_sem=binc_send.at[b],
            recv_sem=binc_recv.at[b], device_id=to_prev, device_id_type=MESH,
        )

    def halo_copy(side, i):
        near, far, dev = (BAND + i, BAND + n + i, to_left) if side == 0 else (n + i, i, to_right)
        return pltpu.make_async_remote_copy(
            src_ref=ext.at[near], dst_ref=ext.at[far], send_sem=halo_send.at[side, i],
            recv_sem=halo_recv.at[side, i], device_id=dev, device_id_type=MESH,
        )

    def rim_copy(side, i):
        return pltpu.make_async_remote_copy(
            src_ref=rim_snd.at[side, i], dst_ref=rim_rcv.at[side, i],
            send_sem=rim_send.at[side, i], recv_sem=rim_recv.at[side, i],
            device_id=(to_left, to_right)[side], device_id_type=MESH,
        )

    for p in range(n):
        src_copy(down_block(p, n)).start()

    @pl.loop(0, slots)
    def _(s):
        tile_copy(s).start()

    barrier = pltpu.get_barrier_semaphore()
    for there, dev in partners:
        @pl.when(there)
        def _(dev=dev):
            pl.semaphore_signal(barrier, inc=1, device_id=dev, device_id_type=MESH)
    pl.semaphore_wait(barrier, sum(there.astype(jnp.int32) for there, _ in partners))

    def product(x, s, dim, write):
        both = jnp.concatenate(
            [x.reshape(2 * half, tile), jnp.concatenate([-x[1], x[0]], axis=0)], axis=1
        )
        if dim == 1:
            matrix = jnp.concatenate([tiles[s, 0], tiles[s, 1]], axis=1)
        else:
            matrix = tiles[s].reshape(2 * tile, tile)
        numbers = (((1,), (dim,)), ((), ()))
        y = lax.dot_general(both, matrix, numbers, preferred_element_type=jnp.float32)
        write(slice(None), y)

    @pl.when(jnp.logical_not(has_left))
    def _():
        ext[0:BAND] = jnp.zeros((BAND,) + ext.shape[1:], ext.dtype)
        rim_rcv[1] = jnp.zeros(rim_rcv.shape[1:], rim_rcv.dtype)

    @pl.when(jnp.logical_not(has_right))
    def _():
        ext[BAND + n:] = jnp.zeros((BAND,) + ext.shape[1:], ext.dtype)
        rim_rcv[0] = jnp.zeros(rim_rcv.shape[1:], rim_rcv.dtype)

    acc[zero] = jnp.zeros(acc.shape[1:], acc.dtype)

    def keep(place):
        def write(at, y):
            acc[place, :, at] = y

        return write

    def chunked(total, slot, after, first=0):
        @pl.loop(first, total // CHUNK)
        def _(p):
            for j in range(CHUNK):
                slot(p * CHUNK + j)
            after(p)

        for k in range(total // CHUNK * CHUNK, total):
            slot(k)

    border = min(n, 2 * BAND)

    def down_arrival(p):
        b = down_block(p, n)
        src_copy(b).wait()

        @pl.when(has_prev)
        def _():
            fwd_copy(b).wait_recv()
            total = src[b].astype(jnp.float32) + inc[b].astype(jnp.float32)
            ext[BAND + b] = total.astype(jnp.bfloat16)

        @pl.when(jnp.logical_not(has_prev))
        def _():
            ext[BAND + b] = src[b]

        down_copy(b).start()

    def down_diagonal(p):
        b = down_block(p, n)
        product(ext[BAND + b], idx[o_table + b * SPAN + BAND], 1, keep(b))

    @pl.loop(0, border)
    def _(p):
        b = down_block(p, n)
        down_arrival(p)

        @pl.when(has_next & has_right & (b >= n - BAND))
        def _():
            halo_copy(1, b - (n - BAND)).start()

        @pl.when(has_next & has_left & (b < BAND))
        def _():
            halo_copy(0, b).start()

    @pl.loop(0, slots)
    def _(s):
        tile_copy(s).wait()

    @pl.when(has_next)
    def _():
        pl.loop(0, border)(down_diagonal)

    @pl.loop(border, n)
    def _(p):
        down_arrival(p)

        @pl.when(has_next)
        def _():
            down_diagonal(p)

    @pl.when(has_next)
    def _():
        for side, there in enumerate((has_right, has_left)):
            @pl.when(there)
            def _(side=side):
                for i in range(BAND):
                    halo_copy(side, i).wait_recv()

        def slot(k):
            product(ext[idx[o_dcol + k]], idx[o_dord + k], 1, keep(n + k))

        def send(p):
            b = down_block(p, n)
            total = acc[b]
            for d in range(SPAN):
                if d != BAND:
                    total = total + acc[idx[o_dat + b * SPAN + d]]
            snd[b] = total.astype(jnp.bfloat16).reshape(snd.shape[1:])
            fwd_copy(b).start()

        chunked(slots - n, slot, send)
        pl.loop((slots - n) // CHUNK, n)(send)

    early = up_early(n)

    def up_diagonal(b):
        product(up[b], idx[o_table + b * SPAN + BAND], 0, keep(b))

    def up_arrival(p):
        b = up_block(p, n)

        @pl.when(has_next)
        def _():
            bwd_copy(b).wait_recv()
            total = ext[BAND + b].astype(jnp.float32) + binc[b].astype(jnp.float32)
            up[b] = total.astype(jnp.bfloat16)

        @pl.when(jnp.logical_not(has_next))
        def _():
            up[b] = ext[BAND + b]

        up_copy(b).start()

        @pl.when(has_prev & has_next)
        def _():
            up_diagonal(b)

    pl.loop(0, early + border)(up_arrival)

    def rim_pair(j):
        low, high = j // 2, n - BAND + (BAND + 1 - j) // 2
        product(up[low], idx[o_table + low * SPAN + j % 2], 0, keep(n + j))
        product(
            up[high], idx[o_table + high * SPAN + SPAN - 1 - j % 2], 0,
            keep(n + RIMS - 1 - j),
        )

    def rim_start(side, b):
        c = b - BAND if side == 0 else n + b
        near = [r for r in range(n) if abs(c - r) <= BAND]
        total = sum(acc[idx[o_uat + r * SPAN + c - r + BAND]] for r in near)
        rim_snd[side, b] = total.astype(jnp.bfloat16).reshape(rim_snd.shape[2:])

        @pl.when((has_left, has_right)[side])
        def _():
            rim_copy(side, b).start()

    def later_rims():
        pl.loop(1, RIMS // 2)(rim_pair)
        rim_start(0, 1)
        rim_start(1, 0)

    rims_first = layer % 2 == 1

    @pl.when(has_prev)
    def _():
        rim_pair(0)
        rim_start(0, 0)
        rim_start(1, 1)

        @pl.when(rims_first)
        def _():
            later_rims()

    pl.loop(early + border, n)(up_arrival)

    @pl.when(has_prev & jnp.logical_not(has_next))
    def _():
        pl.loop(0, n)(up_diagonal)

    @pl.when(has_prev)
    def _():
        def slot(k):
            product(up[idx[o_urow + k]], idx[o_uord + k], 0, keep(n + RIMS + k))

        def summed(b):
            total = acc[b]
            for r in range(-BAND, SPAN - BAND):
                if r != 0:
                    at = (b + r) * SPAN - r + BAND
                    inside = (b + r >= 0) & (b + r < n)
                    place = idx[o_uat + jnp.clip(at, 0, n * SPAN - 1)]
                    total = total + acc[jnp.where(inside, place, zero)]
            return total.reshape(bsnd.shape[1:])

        def send_inside(p):
            b = up_block(p, n)
            bsnd[b] = summed(b).astype(jnp.bfloat16)
            bwd_copy(b).start()

        def after(p):
            @pl.when(p < early)
            def _():
                send_inside(p)

        first = min(1, rest // CHUNK)
        for k in range(first * CHUNK):
            slot(k)
        if first and early:
            send_inside(0)

        @pl.when(jnp.logical_not(rims_first))
        def _():
            later_rims()

        chunked(rest, slot, after, first)
        pl.loop(min(early, rest // CHUNK), early)(send_inside)
        for side, there in enumerate((has_right, has_left)):
            @pl.when(there)
            def _(side=side):
                for i in range(BAND):
                    rim_copy(side, i).wait_recv()
        for p in range(early, early + border):
            b = up_block(p, n)
            total = summed(b)
            if b < BAND:
                total = total + rim_rcv[1, b].astype(jnp.float32)
            if b >= n - BAND:
                total = total + rim_rcv[0, b - (n - BAND)].astype(jnp.float32)
            bsnd[b] = total.astype(jnp.bfloat16)
            bwd_copy(b).start()
        pl.loop(early + border, n)(send_inside)

    for b in range(n):
        down_copy(b).wait()
        up_copy(b).wait()

        @pl.when(has_next)
        def _(b=b):
            fwd_copy(b).wait_send()

        @pl.when(has_prev)
        def _(b=b):
            bwd_copy(b).wait_send()
    for side, there in enumerate((has_left, has_right)):
        @pl.when(has_next & there)
        def _(side=side):
            for i in range(BAND):
                halo_copy(side, i).wait_send()

        @pl.when(has_prev & there)
        def _(side=side):
            for i in range(BAND):
                rim_copy(side, i).wait_send()


def on_device(source, tile_data, tile_rows, tile_cols, tile_count):
    layers, groups = lax.axis_size("layer"), lax.axis_size("blk")
    slots, tile = tile_data.shape[1], tile_data.shape[3]
    _, parts, half, length = source.shape
    n = length // tile
    rest = slots - n - min(1, groups - 1)
    first_block = lax.axis_index("blk") * n
    idx, offsets = plan(tile_rows[0], tile_cols[0], tile_count[0, 0], first_block, n, rest)
    block = (parts, half, tile)
    bf16 = jnp.bfloat16
    dma = pltpu.SemaphoreType.DMA
    shape = jax.ShapeDtypeStruct((parts, half, length), bf16)
    down, up = pl.pallas_call(
        functools.partial(kernel, layers, groups, n, slots, rest, offsets),
        out_shape=(shape, shape),
        in_specs=[
            pl.BlockSpec(memory_space=pltpu.SMEM),
            pl.BlockSpec(memory_space=pl.ANY),
            pl.BlockSpec(memory_space=pl.ANY),
        ],
        out_specs=(pl.BlockSpec(memory_space=pl.ANY), pl.BlockSpec(memory_space=pl.ANY)),
        scratch_shapes=[
            pltpu.VMEM((slots, 2, tile, tile), bf16),
            pltpu.VMEM((max(slots, n + RIMS + rest) + 1, parts * half, tile), jnp.float32),
            pltpu.VMEM((n,) + block, bf16),
            pltpu.VMEM((n + 2 * BAND,) + block, bf16),
            pltpu.VMEM((n,) + block, bf16),
            pltpu.VMEM((n,) + block, bf16),
            pltpu.VMEM((n,) + block, bf16),
            pltpu.VMEM((n,) + block, bf16),
            pltpu.VMEM((n,) + block, bf16),
            pltpu.VMEM((2, BAND) + block, bf16),
            pltpu.VMEM((2, BAND) + block, bf16),
            dma((slots,)),
            dma((n,)),
            dma((2, n)),
            dma((n,)),
            dma((n,)),
            dma((n,)),
            dma((n,)),
            dma((2, BAND)),
            dma((2, BAND)),
            dma((2, BAND)),
            dma((2, BAND)),
        ],
        compiler_params=pltpu.CompilerParams(
            collective_id=0, has_side_effects=True, vmem_limit_bytes=62 * 1024 * 1024
        ),
    )(idx, source[0], tile_data[0])
    return (down[None], up[None])


def solution(mesh):
    in_specs = (
        P("layer", None, None, "blk"),
        P("layer", "blk", None, None, None),
        P("layer", "blk"),
        P("layer", "blk"),
        P("layer", "blk"),
    )
    out_specs = (P("layer", None, None, "blk"), P("layer", None, None, "blk"))
    return jax.shard_map(
        on_device, mesh=mesh, in_specs=in_specs, out_specs=out_specs, check_vma=False
    )
```

```python
import functools

import jax
import jax.numpy as jnp
from jax import lax
from jax.experimental import pallas as pl
from jax.experimental.pallas import tpu as pltpu
from jax.sharding import PartitionSpec as P

BAND = 2
MESH = pl.DeviceIdType.MESH


SPAN = 2 * BAND + 1
RIMS = BAND * (BAND + 1)
CHUNK = 2 * BAND


def down_block(p, n):
    return (p + n - BAND) % n


def up_early(n):
    return max(0, (n - 2 * BAND) // 2)


def up_block(p, n):
    return (p + n - BAND - up_early(n)) % n


def sorted_by(key, values):
    slots = key.shape[0]
    rank = jnp.sum(key[None, :] < key[:, None], axis=1).astype(jnp.int32)
    place = rank[None, :] == jnp.arange(slots)[:, None]
    return rank, jnp.sum(jnp.where(place[None], values[:, None, :], 0), axis=2)


def plan(rows, cols, count, first_block, n, rest):
    slots = rows.shape[0]
    ids = jnp.arange(slots, dtype=jnp.int32)
    r = rows - first_block
    c = cols - first_block
    live = ids < count
    diag = live & (c == r)
    left, right = c < 0, c >= n
    rim = live & (left | right)
    big = n * slots
    key = jnp.where(live, ((r + BAND) % n) * slots, big) + ids
    key = jnp.where(diag, key + 2 * big, key)
    rank, (d_ord, d_col) = sorted_by(key, jnp.stack([ids, c + BAND]))
    d_pos = jnp.where(diag, r, n + rank)
    key = jnp.where(live, ((c + BAND + up_early(n)) % n) * slots, big) + ids
    key = jnp.where(diag | rim, key + 2 * big, key)
    rank, (u_ord, u_row) = sorted_by(key, jnp.stack([ids, r]))
    rim_at = jnp.where(left, r + c + BAND, RIMS // 2 + r + BAND - n + c - n)
    u_pos = jnp.where(diag, r, n + jnp.where(rim, rim_at, RIMS + rank))
    zero = max(slots, n + RIMS + rest)
    place = r * SPAN + c - r + BAND
    match = live[:, None] & (place[:, None] == jnp.arange(n * SPAN)[None, :])
    values = jnp.stack([ids, d_pos - zero, u_pos - zero])
    table, d_at, u_at = jnp.sum(jnp.where(match[None], values[:, :, None], 0), axis=1)
    parts = [table, d_at + zero, u_at + zero, d_ord, d_col, u_ord, u_row]
    offsets, at = [], 0
    for p in parts:
        offsets.append(at)
        at += p.shape[0]
    return jnp.concatenate([p.astype(jnp.int32) for p in parts]), offsets


def kernel(
    layers, groups, n, slots, rest, offsets,
    idx, source, tiles_hbm, down_out, up_out,
    tiles, acc, src, ext, up, inc, binc, snd, bsnd, rim_snd, rim_rcv,
    tile_sem, src_sem, out_sem, inc_send, inc_recv, binc_send, binc_recv,
    halo_send, halo_recv, rim_send, rim_recv,
):
    o_table, o_dat, o_uat, o_dord, o_dcol, o_uord, o_urow = offsets
    zero = acc.shape[0] - 1
    half, tile = src.shape[2], src.shape[3]
    layer = lax.axis_index("layer")
    blk = lax.axis_index("blk")
    has_prev, has_next = layer > 0, layer < layers - 1
    has_left, has_right = blk > 0, blk < groups - 1
    to_prev, to_next = (layer - 1, blk), (layer + 1, blk)
    to_left, to_right = (layer, blk - 1), (layer, blk + 1)
    partners = ((has_prev, to_prev), (has_next, to_next), (has_left, to_left), (has_right, to_right))

    def tile_copy(s):
        return pltpu.make_async_copy(tiles_hbm.at[s], tiles.at[s], tile_sem.at[s])

    def src_copy(b):
        return pltpu.make_async_copy(
            source.at[:, :, pl.ds(b * tile, tile)], src.at[b], src_sem.at[b]
        )

    def down_copy(b):
        return pltpu.make_async_copy(
            ext.at[BAND + b], down_out.at[:, :, pl.ds(b * tile, tile)], out_sem.at[0, b]
        )

    def up_copy(b):
        return pltpu.make_async_copy(
            up.at[b], up_out.at[:, :, pl.ds(b * tile, tile)], out_sem.at[1, b]
        )

    def fwd_copy(b):
        return pltpu.make_async_remote_copy(
            src_ref=snd.at[b], dst_ref=inc.at[b], send_sem=inc_send.at[b],
            recv_sem=inc_recv.at[b], device_id=to_next, device_id_type=MESH,
        )

    def bwd_copy(b):
        return pltpu.make_async_remote_copy(
            src_ref=bsnd.at[b], dst_ref=binc.at[b], send_sem=binc_send.at[b],
            recv_sem=binc_recv.at[b], device_id=to_prev, device_id_type=MESH,
        )

    def halo_copy(side, i):
        near, far, dev = (BAND + i, BAND + n + i, to_left) if side == 0 else (n + i, i, to_right)
        return pltpu.make_async_remote_copy(
            src_ref=ext.at[near], dst_ref=ext.at[far], send_sem=halo_send.at[side, i],
            recv_sem=halo_recv.at[side, i], device_id=dev, device_id_type=MESH,
        )

    def rim_copy(side, i):
        return pltpu.make_async_remote_copy(
            src_ref=rim_snd.at[side, i], dst_ref=rim_rcv.at[side, i],
            send_sem=rim_send.at[side, i], recv_sem=rim_recv.at[side, i],
            device_id=(to_left, to_right)[side], device_id_type=MESH,
        )

    for p in range(n):
        src_copy(down_block(p, n)).start()

    @pl.loop(0, slots)
    def _(s):
        tile_copy(s).start()

    barrier = pltpu.get_barrier_semaphore()
    for there, dev in partners:
        @pl.when(there)
        def _(dev=dev):
            pl.semaphore_signal(barrier, inc=1, device_id=dev, device_id_type=MESH)
    pl.semaphore_wait(barrier, sum(there.astype(jnp.int32) for there, _ in partners))

    def product(x, s, dim, write):
        both = jnp.concatenate(
            [x.reshape(2 * half, tile), jnp.concatenate([-x[1], x[0]], axis=0)], axis=1
        )
        if dim == 1:
            matrix = jnp.concatenate([tiles[s, 0], tiles[s, 1]], axis=1)
        else:
            matrix = tiles[s].reshape(2 * tile, tile)
        numbers = (((1,), (dim,)), ((), ()))
        y = lax.dot_general(both, matrix, numbers, preferred_element_type=jnp.float32)
        write(slice(None), y)

    @pl.when(jnp.logical_not(has_left))
    def _():
        ext[0:BAND] = jnp.zeros((BAND,) + ext.shape[1:], ext.dtype)
        rim_rcv[1] = jnp.zeros(rim_rcv.shape[1:], rim_rcv.dtype)

    @pl.when(jnp.logical_not(has_right))
    def _():
        ext[BAND + n:] = jnp.zeros((BAND,) + ext.shape[1:], ext.dtype)
        rim_rcv[0] = jnp.zeros(rim_rcv.shape[1:], rim_rcv.dtype)

    acc[zero] = jnp.zeros(acc.shape[1:], acc.dtype)

    def keep(place):
        def write(at, y):
            acc[place, :, at] = y

        return write

    def chunked(total, slot, after, first=0):
        @pl.loop(first, total // CHUNK)
        def _(p):
            for j in range(CHUNK):
                slot(p * CHUNK + j)
            after(p)

        for k in range(total // CHUNK * CHUNK, total):
            slot(k)

    border = min(n, 2 * BAND)

    def down_arrival(p):
        b = down_block(p, n)
        src_copy(b).wait()

        @pl.when(has_prev)
        def _():
            fwd_copy(b).wait_recv()
            total = src[b].astype(jnp.float32) + inc[b].astype(jnp.float32)
            ext[BAND + b] = total.astype(jnp.bfloat16)

        @pl.when(jnp.logical_not(has_prev))
        def _():
            ext[BAND + b] = src[b]

        down_copy(b).start()

    def down_diagonal(p):
        b = down_block(p, n)
        product(ext[BAND + b], idx[o_table + b * SPAN + BAND], 1, keep(b))

    @pl.loop(0, border)
    def _(p):
        b = down_block(p, n)
        down_arrival(p)

        @pl.when(has_next & has_right & (b >= n - BAND))
        def _():
            halo_copy(1, b - (n - BAND)).start()

        @pl.when(has_next & has_left & (b < BAND))
        def _():
            halo_copy(0, b).start()

    @pl.loop(0, slots)
    def _(s):
        tile_copy(s).wait()

    @pl.when(has_next)
    def _():
        pl.loop(0, border)(down_diagonal)

    @pl.loop(border, n)
    def _(p):
        down_arrival(p)

        @pl.when(has_next)
        def _():
            down_diagonal(p)

    @pl.when(has_next)
    def _():
        for side, there in enumerate((has_right, has_left)):
            @pl.when(there)
            def _(side=side):
                for i in range(BAND):
                    halo_copy(side, i).wait_recv()

        def slot(k):
            product(ext[idx[o_dcol + k]], idx[o_dord + k], 1, keep(n + k))

        def send(p):
            b = down_block(p, n)
            total = acc[b]
            for d in range(SPAN):
                if d != BAND:
                    total = total + acc[idx[o_dat + b * SPAN + d]]
            snd[b] = total.astype(jnp.bfloat16).reshape(snd.shape[1:])
            fwd_copy(b).start()

        chunked(slots - n, slot, send)
        pl.loop((slots - n) // CHUNK, n)(send)

    early = up_early(n)

    def up_diagonal(b):
        product(up[b], idx[o_table + b * SPAN + BAND], 0, keep(b))

    def up_arrival(p):
        b = up_block(p, n)

        @pl.when(has_next)
        def _():
            bwd_copy(b).wait_recv()
            total = ext[BAND + b].astype(jnp.float32) + binc[b].astype(jnp.float32)
            up[b] = total.astype(jnp.bfloat16)

        @pl.when(jnp.logical_not(has_next))
        def _():
            up[b] = ext[BAND + b]

        up_copy(b).start()

        @pl.when(has_prev & has_next)
        def _():
            up_diagonal(b)

    pl.loop(0, early + border)(up_arrival)

    def rim_pair(j):
        low, high = j // 2, n - BAND + (BAND + 1 - j) // 2
        product(up[low], idx[o_table + low * SPAN + j % 2], 0, keep(n + j))
        product(
            up[high], idx[o_table + high * SPAN + SPAN - 1 - j % 2], 0,
            keep(n + RIMS - 1 - j),
        )

    def rim_start(side, b):
        c = b - BAND if side == 0 else n + b
        near = [r for r in range(n) if abs(c - r) <= BAND]
        total = sum(acc[idx[o_uat + r * SPAN + c - r + BAND]] for r in near)
        rim_snd[side, b] = total.astype(jnp.bfloat16).reshape(rim_snd.shape[2:])

        @pl.when((has_left, has_right)[side])
        def _():
            rim_copy(side, b).start()

    def later_rims():
        pl.loop(1, RIMS // 2)(rim_pair)
        rim_start(0, 1)
        rim_start(1, 0)

    rims_first = layer % 2 == 1

    @pl.when(has_prev)
    def _():
        rim_pair(0)
        rim_start(0, 0)
        rim_start(1, 1)

        @pl.when(rims_first)
        def _():
            later_rims()

    pl.loop(early + border, n)(up_arrival)

    @pl.when(has_prev & jnp.logical_not(has_next))
    def _():
        pl.loop(0, n)(up_diagonal)

    @pl.when(has_prev)
    def _():
        def slot(k):
            product(up[idx[o_urow + k]], idx[o_uord + k], 0, keep(n + RIMS + k))

        def summed(b):
            total = acc[b]
            for r in range(-BAND, SPAN - BAND):
                if r != 0:
                    at = (b + r) * SPAN - r + BAND
                    inside = (b + r >= 0) & (b + r < n)
                    place = idx[o_uat + jnp.clip(at, 0, n * SPAN - 1)]
                    total = total + acc[jnp.where(inside, place, zero)]
            return total.reshape(bsnd.shape[1:])

        def send_inside(p):
            b = up_block(p, n)
            bsnd[b] = summed(b).astype(jnp.bfloat16)
            bwd_copy(b).start()

        def after(p):
            @pl.when(p < early)
            def _():
                send_inside(p)

        first = min(1, rest // CHUNK)
        for k in range(first * CHUNK):
            slot(k)
        if first and early:
            send_inside(0)

        @pl.when(jnp.logical_not(rims_first))
        def _():
            later_rims()

        chunked(rest, slot, after, first)
        pl.loop(min(early, rest // CHUNK), early)(send_inside)
        for side, there in enumerate((has_right, has_left)):
            @pl.when(there)
            def _(side=side):
                for i in range(BAND):
                    rim_copy(side, i).wait_recv()
        for p in range(early, early + border):
            b = up_block(p, n)
            total = summed(b)
            if b < BAND:
                total = total + rim_rcv[1, b].astype(jnp.float32)
            if b >= n - BAND:
                total = total + rim_rcv[0, b - (n - BAND)].astype(jnp.float32)
            bsnd[b] = total.astype(jnp.bfloat16)
            bwd_copy(b).start()
        pl.loop(early + border, n)(send_inside)

    for b in range(n):
        down_copy(b).wait()
        up_copy(b).wait()

        @pl.when(has_next)
        def _(b=b):
            fwd_copy(b).wait_send()

        @pl.when(has_prev)
        def _(b=b):
            bwd_copy(b).wait_send()
    for side, there in enumerate((has_left, has_right)):
        @pl.when(has_next & there)
        def _(side=side):
            for i in range(BAND):
                halo_copy(side, i).wait_send()

        @pl.when(has_prev & there)
        def _(side=side):
            for i in range(BAND):
                rim_copy(side, i).wait_send()


def on_device(source, tile_data, tile_rows, tile_cols, tile_count):
    layers, groups = lax.axis_size("layer"), lax.axis_size("blk")
    slots, tile = tile_data.shape[1], tile_data.shape[3]
    _, parts, half, length = source.shape
    n = length // tile
    rest = slots - n - min(1, groups - 1)
    first_block = lax.axis_index("blk") * n
    idx, offsets = plan(tile_rows[0], tile_cols[0], tile_count[0, 0], first_block, n, rest)
    block = (parts, half, tile)
    bf16 = jnp.bfloat16
    dma = pltpu.SemaphoreType.DMA
    shape = jax.ShapeDtypeStruct((parts, half, length), bf16)
    down, up = pl.pallas_call(
        functools.partial(kernel, layers, groups, n, slots, rest, offsets),
        out_shape=(shape, shape),
        in_specs=[
            pl.BlockSpec(memory_space=pltpu.SMEM),
            pl.BlockSpec(memory_space=pl.ANY),
            pl.BlockSpec(memory_space=pl.ANY),
        ],
        out_specs=(pl.BlockSpec(memory_space=pl.ANY), pl.BlockSpec(memory_space=pl.ANY)),
        scratch_shapes=[
            pltpu.VMEM((slots, 2, tile, tile), bf16),
            pltpu.VMEM((max(slots, n + RIMS + rest) + 1, parts * half, tile), jnp.float32),
            pltpu.VMEM((n,) + block, bf16),
            pltpu.VMEM((n + 2 * BAND,) + block, bf16),
            pltpu.VMEM((n,) + block, bf16),
            pltpu.VMEM((n,) + block, bf16),
            pltpu.VMEM((n,) + block, bf16),
            pltpu.VMEM((n,) + block, bf16),
            pltpu.VMEM((n,) + block, bf16),
            pltpu.VMEM((2, BAND) + block, bf16),
            pltpu.VMEM((2, BAND) + block, bf16),
            dma((slots,)),
            dma((n,)),
            dma((2, n)),
            dma((n,)),
            dma((n,)),
            dma((n,)),
            dma((n,)),
            dma((2, BAND)),
            dma((2, BAND)),
            dma((2, BAND)),
            dma((2, BAND)),
        ],
        compiler_params=pltpu.CompilerParams(
            collective_id=0, has_side_effects=True, vmem_limit_bytes=62 * 1024 * 1024
        ),
    )(idx, source[0], tile_data[0])
    return (down[None], up[None])


def solution(mesh):
    in_specs = (
        P("layer", None, None, "blk"),
        P("layer", "blk", None, None, None),
        P("layer", "blk"),
        P("layer", "blk"),
        P("layer", "blk"),
    )
    out_specs = (P("layer", None, None, "blk"), P("layer", None, None, "blk"))
    return jax.shard_map(
        on_device, mesh=mesh, in_specs=in_specs, out_specs=out_specs, check_vma=False
    )
```
